256 devices in a mesh: tile: 128 (over x, y_lo, z, core), member: 2 (over y_hi).
Axes of the slice: x: 4, y: 4 (y_hi: 2, y_lo: 2; y = y_hi * 2 + y_lo), z: 8, core: 2. Of those that a mesh axis runs over, the one named last changes fastest.
Arguments:
- inputs: bfloat16 [2, 128, 64, 1024], P('member', 'tile'), may hold values from -6 to 6
- cotangent: bfloat16 [2, 128, 64, 256], P('member', 'tile'), may hold values from -6 to 6
- seam_codes: int32 [128, 4], P('tile'), may hold values from 0 to 3, as said below
- conv_one: bfloat16 [64, 576], replicated, may hold values from -0.25 to 0.25
- conv_two: bfloat16 [64, 576], replicated, may hold values from -0.25 to 0.25
- down_weight: bfloat16 [64, 256], replicated, may hold values from -0.375 to 0.375
Outputs:
- encoded: bfloat16 [2, 128, 64, 256], P('member', 'tile')
- input_grad: bfloat16 [2, 128, 64, 1024], P('member', 'tile')
- conv_one_grad: float32 [64, 576], replicated
- conv_two_grad: float32 [64, 576], replicated
- down_grad: float32 [64, 256], replicated
The draws below stay inside these ranges and needn't reach their ends.
Inputs may be any that keep to these rules, and one draw needn't show every extreme that they name: `seam_codes`: sides inside a face have code 0; across a face border the two sides of one seam carry reciprocal codes c and (4 - c) mod 4, the same along the whole border between two faces.
All inputs are finite; a program needn't handle non-finite values.
Results may differ from the reference program's by a relative error of at most 0.0061.
Values may be sent and summed in bfloat16 or wider, within the bound.
No kernel may reach another device: no remote copies, remote signals or barrier semaphores. Data moves between devices by JAX's collectives and lax.ppermute only.
A program may use at most 64 MiB of HBM per device.

```python
import math
import jax
import jax.numpy as jnp
from jax import lax

C = 64
S = 32
ROW_TILES = 8
TILES = 128
MEMBERS = 2


def draw_seam_codes(key, part):
    key = jax.random.fold_in(key, 7)
    row_count = TILES // ROW_TILES
    face_high = min(4, row_count)
    face_rows = row_count // face_high
    face_cols = ROW_TILES // 4
    east_key, south_key = jax.random.split(key)
    east_codes = jax.random.randint(east_key, (face_rows, face_cols), 1, 4).astype(jnp.int32)
    east_codes = east_codes.at[0, 0].set(1)
    south_codes = jax.random.randint(south_key, (face_rows, face_cols), 1, 4).astype(jnp.int32)
    tile_ids = jnp.arange(TILES, dtype=jnp.int32)

    def east_of(tile_ids):
        row_now = tile_ids // ROW_TILES
        col_now = tile_ids % ROW_TILES
        border = (col_now + 1) % 4 == 0
        return jnp.where(border, east_codes[row_now // face_high, col_now // 4], 0)

    def south_of(tile_ids):
        row_now = tile_ids // ROW_TILES
        col_now = tile_ids % ROW_TILES
        border = (row_now + 1) % face_high == 0
        return jnp.where(border, south_codes[row_now // face_high, col_now // 4], 0)
    east_side = east_of(tile_ids)
    south_side = south_of(tile_ids)
    west_side = (4 - east_of((tile_ids - 1) % TILES)) % 4
    north_side = (4 - south_of((tile_ids - ROW_TILES) % TILES)) % 4
    return jnp.stack([north_side, east_side, south_side, west_side], axis=1).astype(jnp.int32)


def level_of(rng, extent, cuts, low, high):
    def one(axis_at, shards_of):
        steps = jax.random.uniform(jax.random.fold_in(jax.random.fold_in(rng, 6), axis_at), (shards_of,), jnp.float32, low / len(cuts), high / len(cuts))
        return jnp.repeat(jnp.exp(steps), extent[axis_at] // shards_of).reshape((-1,) + (1,) * (len(extent) - axis_at - 1))

    gain = one(*cuts[0])
    for cut in cuts[1:]:
        gain = gain * one(*cut)
    return gain


def bell_draw(stream_key, dims, width, limit, shards=(), kind=jnp.bfloat16):
    loudness = level_of(stream_key, dims, shards, -0.22, 0.18) if shards else 1.0
    result = jax.random.normal(stream_key, dims, jnp.float32) * width * loudness
    return jnp.minimum(jnp.maximum(result, -limit), limit).astype(kind)


def setup_inputs(seed: int = 0) -> dict:
    arg_keys = jax.random.split(jax.random.key(seed), 7)
    return {
        "inputs": bell_draw(arg_keys[0], (MEMBERS, TILES, C, S * S), 1.0, 6.0, ((0, 2), (1, 128))),
        "cotangent": bell_draw(arg_keys[1], (MEMBERS, TILES, C, S * S // 4), 1.0, 6.0, ((0, 2), (1, 128))),
        "seam_codes": draw_seam_codes(jax.random.fold_in(arg_keys[6], 71), 0),
        "conv_one": bell_draw(arg_keys[3], (C, 9 * C), (9 * C) ** -0.5, 0.25),
        "conv_two": bell_draw(arg_keys[4], (C, 9 * C), (9 * C) ** -0.5, 0.25),
        "down_weight": bell_draw(arg_keys[5], (C, 4 * C), (4 * C) ** -0.5, 0.375),
    }


def strips(field, rim_width):
    north = field[..., :rim_width, :]
    east = jnp.swapaxes(jnp.flip(field[..., :, -rim_width:], -1), -1, -2)
    south = jnp.flip(field[..., -rim_width:, :], -2)
    west = jnp.swapaxes(field[..., :, :rim_width], -1, -2)
    return jnp.stack([north, east, south, west], axis=-4)

def assemble(field, sides, corner_blocks, rim_width):
    north_east, north_west, south_east, south_west = corner_blocks
    top_rows = jnp.concatenate([north_west, jnp.flip(sides[0], -2), north_east], axis=-1)
    middle = jnp.concatenate([jnp.swapaxes(jnp.flip(sides[3], -2), -1, -2), field, jnp.swapaxes(sides[1], -1, -2)], axis=-1)
    bottom_rows = jnp.concatenate([south_west, sides[2], south_east], axis=-1)
    return jnp.concatenate([top_rows, middle, bottom_rows], axis=-2)

def edge_grads(grad_pad, rim_width):
    inner = grad_pad.shape[-1] - rim_width
    north = jnp.flip(grad_pad[..., :rim_width, rim_width:inner], -2)
    south = grad_pad[..., inner:, rim_width:inner]
    west = jnp.flip(jnp.swapaxes(grad_pad[..., rim_width:inner, :rim_width], -1, -2), -2)
    east = jnp.swapaxes(grad_pad[..., rim_width:inner, inner:], -1, -2)
    corner_blocks = (grad_pad[..., :rim_width, inner:], grad_pad[..., :rim_width, :rim_width], grad_pad[..., inner:, inner:], grad_pad[..., inner:, :rim_width])
    return ([north, east, south, west], corner_blocks)

def add_strips(grads, stacked, rim_width):
    grads = grads.at[..., :rim_width, :].add(stacked[..., 0, :, :, :])
    grads = grads.at[..., :, -rim_width:].add(jnp.flip(jnp.swapaxes(stacked[..., 1, :, :, :], -1, -2), -1))
    grads = grads.at[..., -rim_width:, :].add(jnp.flip(stacked[..., 2, :, :, :], -2))
    grads = grads.at[..., :, :rim_width].add(jnp.swapaxes(stacked[..., 3, :, :, :], -1, -2))
    return grads

def extend_all(field, rim_width, seam_codes, offsets):
    edge_stack = strips(field, rim_width)
    sides = []
    for direction in range(4):
        neighbour_stack = jnp.roll(edge_stack, -offsets[direction], axis=0)
        code_now = seam_codes[:, direction]
        chosen = (code_now + direction + 2) % 4
        onehot = jnp.arange(4, dtype=jnp.int32)[None, :] == chosen[:, None]
        picked = lax.optimization_barrier(jnp.sum(jnp.where(onehot[:, :, None, None, None], neighbour_stack, jnp.zeros((), neighbour_stack.dtype)), axis=1))
        flipped = (code_now % 2 == 1)[:, None, None, None]
        sides.append(jnp.where(flipped, jnp.flip(picked, -1), picked))
    north_east = jnp.roll(field[:, :, -rim_width:, :rim_width], ROW_TILES - 1, axis=0)
    north_west = jnp.roll(field[:, :, -rim_width:, -rim_width:], ROW_TILES + 1, axis=0)
    south_east = jnp.roll(field[:, :, :rim_width, :rim_width], -(ROW_TILES + 1), axis=0)
    south_west = jnp.roll(field[:, :, :rim_width, -rim_width:], -(ROW_TILES - 1), axis=0)
    return assemble(field, sides, (north_east, north_west, south_east, south_west), rim_width)

def retract_all(grad_pad, rim_width, seam_codes, offsets):
    inner = grad_pad.shape[-1] - rim_width
    grads = grad_pad[:, :, rim_width:inner, rim_width:inner]
    sides, corner_blocks = edge_grads(grad_pad, rim_width)
    total = jnp.zeros((grads.shape[0], 4) + sides[0].shape[1:], grads.dtype)
    for direction in range(4):
        code_now = seam_codes[:, direction]
        chosen = (code_now + direction + 2) % 4
        onehot = jnp.arange(4, dtype=jnp.int32)[None, :] == chosen[:, None]
        flipped = (code_now % 2 == 1)[:, None, None, None]
        oriented = jnp.where(flipped, jnp.flip(sides[direction], -1), sides[direction])
        placed = jnp.where(onehot[:, :, None, None, None], oriented[:, None], jnp.zeros((), grads.dtype))
        total = total + jnp.roll(placed, offsets[direction], axis=0)
    grads = add_strips(grads, total, rim_width)
    grads = grads.at[:, :, -rim_width:, :rim_width].add(jnp.roll(corner_blocks[0], 1 - ROW_TILES, axis=0))
    grads = grads.at[:, :, -rim_width:, -rim_width:].add(jnp.roll(corner_blocks[1], -(ROW_TILES + 1), axis=0))
    grads = grads.at[:, :, :rim_width, :rim_width].add(jnp.roll(corner_blocks[2], ROW_TILES + 1, axis=0))
    grads = grads.at[:, :, :rim_width, -rim_width:].add(jnp.roll(corner_blocks[3], ROW_TILES - 1, axis=0))
    return grads

def conv_forward(padded, kernel, dilation):
    return lax.conv_general_dilated(padded.astype(jnp.float32), kernel.astype(jnp.float32), (1, 1), 'VALID', rhs_dilation=(dilation, dilation), dimension_numbers=('NCHW', 'OIHW', 'NCHW'), precision=lax.Precision.HIGHEST)

def conv_adjoint(delta, kernel, dilation):
    flipped = jnp.transpose(jnp.flip(kernel, (2, 3)), (1, 0, 2, 3))
    margin = 2 * dilation
    return lax.conv_general_dilated(delta.astype(jnp.float32), flipped.astype(jnp.float32), (1, 1), ((margin, margin), (margin, margin)), rhs_dilation=(dilation, dilation), dimension_numbers=('NCHW', 'OIHW', 'NCHW'), precision=lax.Precision.HIGHEST)

def conv_weight_grad(delta, padded, dilation):
    pieces = []
    delta_wide = delta.astype(jnp.float32)
    for row_tap in range(3):
        for col_tap in range(3):
            window = padded[:, :, row_tap * dilation:row_tap * dilation + S, col_tap * dilation:col_tap * dilation + S].astype(jnp.float32)
            pieces.append(jnp.einsum('toyx,tiyx->oi', delta_wide, window, precision=lax.Precision.HIGHEST))
    return jnp.concatenate(pieces, axis=1)

def gelu_back(preact, upstream):
    return jax.vjp(jax.nn.gelu, preact)[1](upstream)[0]

def reference(inputs, cotangent, seam_codes, conv_one, conv_two, down_weight):
    offsets = (-ROW_TILES, 1, ROW_TILES, -1)
    kernel_one = jnp.transpose(conv_one.reshape(C, 3, 3, C), (0, 3, 1, 2))
    kernel_two = jnp.transpose(conv_two.reshape(C, 3, 3, C), (0, 3, 1, 2))
    down_kernel = jnp.transpose(down_weight.reshape(C, 2, 2, C), (0, 3, 1, 2))
    grad_one_sum = jnp.zeros((C, 9 * C), jnp.float32)
    grad_two_sum = jnp.zeros((C, 9 * C), jnp.float32)
    grad_down_sum = jnp.zeros((C, 4 * C), jnp.float32)
    encoded_list = []
    input_list = []
    half = S // 2
    for member in range(MEMBERS):
        state = inputs[member].reshape(TILES, C, S, S)
        upstream = cotangent[member].reshape(TILES, C, half, half)
        padded_in = extend_all(state, 1, seam_codes, offsets)
        pre_one = conv_forward(padded_in, kernel_one, 1)
        hidden_one = jax.nn.gelu(pre_one).astype(jnp.bfloat16)
        padded_mid = extend_all(hidden_one, 2, seam_codes, offsets)
        pre_two = conv_forward(padded_mid, kernel_two, 2)
        hidden_two = jax.nn.gelu(pre_two).astype(jnp.bfloat16)
        encoded = lax.conv_general_dilated(hidden_two.astype(jnp.float32), down_kernel.astype(jnp.float32), (2, 2), 'VALID', dimension_numbers=('NCHW', 'OIHW', 'NCHW'), precision=lax.Precision.HIGHEST)
        encoded_list.append(encoded.astype(jnp.bfloat16).reshape(TILES, C, half * half))
        grad_two = jnp.einsum('oiab,toyx->tiyaxb', down_kernel.astype(jnp.float32), upstream.astype(jnp.float32), precision=lax.Precision.HIGHEST).reshape(TILES, C, S, S)
        split_two = hidden_two.reshape(TILES, C, half, 2, half, 2).astype(jnp.float32)
        grad_down = jnp.einsum('toyx,tiyaxb->oabi', upstream.astype(jnp.float32), split_two, precision=lax.Precision.HIGHEST).reshape(C, 4 * C)
        delta_two = gelu_back(pre_two, grad_two).astype(jnp.bfloat16)
        grad_conv_two = conv_weight_grad(delta_two, padded_mid, 2)
        grad_mid = retract_all(conv_adjoint(delta_two, kernel_two, 2), 2, seam_codes, offsets)
        delta_one = gelu_back(pre_one, grad_mid).astype(jnp.bfloat16)
        grad_conv_one = conv_weight_grad(delta_one, padded_in, 1)
        grad_input = retract_all(conv_adjoint(delta_one, kernel_one, 1), 1, seam_codes, offsets)
        input_list.append(grad_input.astype(jnp.bfloat16).reshape(TILES, C, S * S))
        grad_one_sum = grad_one_sum + grad_conv_one
        grad_two_sum = grad_two_sum + grad_conv_two
        grad_down_sum = grad_down_sum + grad_down
    scale = 1.0 / math.sqrt(MEMBERS * TILES * S * S)
    return (jnp.stack(encoded_list), jnp.stack(input_list), grad_one_sum * scale, grad_two_sum * scale, grad_down_sum * scale)
```

```python
import math

import jax
import jax.numpy as jnp
from jax import lax
from jax.experimental import pallas as pl
from jax.experimental.pallas import tpu as pltpu
from jax.sharding import PartitionSpec as P

S = 32
C = 64
ROW_TILES = 8
PITCH = 36
BASE = 128
INNER = S * PITCH
FULL = INNER + 2 * BASE
WIDE = FULL + 2 * BASE
SLOT = 128
CORNER = 64
BF = jnp.bfloat16
F32 = jnp.float32


def call(body, outs, scratch, args, flops, name):
    specs = [
        pl.BlockSpec(memory_space=pltpu.SMEM if a.dtype == jnp.int32 else pltpu.VMEM) for a in args
    ]
    moved = sum(math.prod(o.shape) * o.dtype.itemsize for o in list(outs) + list(args))
    return pl.pallas_call(
        body,
        out_shape=outs,
        in_specs=specs,
        out_specs=[pl.BlockSpec(memory_space=pltpu.VMEM)] * len(outs),
        scratch_shapes=scratch,
        compiler_params=pltpu.CompilerParams(vmem_limit_bytes=24 * 2**20),
        cost_estimate=pl.CostEstimate(flops=flops, bytes_accessed=moved, transcendentals=0),
        name=name,
    )(*args)


def out(shape, dtype):
    return jax.ShapeDtypeStruct(shape, dtype)


def nt(a, b):
    return lax.dot_general(a, b, (((1,), (1,)), ((), ())), preferred_element_type=F32)


def mm(a, b):
    return jnp.dot(a, b, preferred_element_type=F32)


def lanes_of():
    lane = lax.broadcasted_iota(jnp.int32, (1, SLOT), 1)
    part = lane - CORNER
    return lane, lane >> 5, lane & 31, part, part >> 2, part & 3


def corner_offsets(j, width):
    if width == 2:
        return j >> 1, j & 1, j >= 0
    return 0 * j, 0 * j, j == 0


def source_row(facts, group, width, pitch, base):
    lane, depth, along, part, kind, j = lanes_of()
    side, code = facts[0, group], facts[0, 4 + group]
    edge = (side - code + 4) & 3
    along = jnp.where((code & 1) == 1, 31 - along, along)
    level = jnp.where(edge >= 2, depth, depth)
    near = jnp.where((edge == 1) | (edge == 2), 31 - level, level)
    rows = (edge & 1) == 0
    y = jnp.where(rows, near, along)
    x = jnp.where(rows, along, near)
    valid = lane < S * width
    if group >= 2:
        u, v, there = corner_offsets(j, width)
        mine = (part >= 0) & (kind < 4) & ((kind & 1) == group - 2) & there
        cy = jnp.where(kind >= 2, S - width + u, u)
        cx = jnp.where(side == 1, S - width + v, v)
        y = jnp.where(mine, cy, y)
        x = jnp.where(mine, cx, x)
        valid = valid | mine
    return jnp.where(valid, base + pitch * y + x, -1)


def rim_row(facts, group, width):
    lane, depth, along, part, kind, j = lanes_of()
    side, second = facts[0, group], facts[0, 2]
    beyond = jnp.where((side == 0) | (side == 3), -1 - depth, S + depth)
    rows = (side & 1) == 0
    y = jnp.where(rows, beyond, along)
    x = jnp.where(rows, along, beyond)
    valid = lane < S * width
    if group < 2:
        u, v, there = corner_offsets(j, width)
        south = jnp.where(side == 0, 1, 0)
        mine = (part >= 0) & (kind < 4) & ((kind >> 1) == south) & there
        east = jnp.where((kind & 1) == 0, second, 4 - second) == 1
        cy = jnp.where(side == 0, u - width, S + u)
        cx = jnp.where(east, S + v, v - width)
        y = jnp.where(mine, cy, y)
        x = jnp.where(mine, cx, x)
        valid = valid | mine
    return jnp.where(valid, BASE + PITCH * y + x, -1)


def pick(rows, start, count):
    row = jnp.concatenate(rows, axis=1)
    place = start + lax.broadcasted_iota(jnp.int32, (count, row.shape[1]), 0)
    return jnp.where(place == row, 1.0, 0.0).astype(BF)


def sources(facts, width, pitch=PITCH, base=BASE):
    return [source_row(facts, g, width, pitch, base) for g in range(4)]


def rims(facts, width):
    return [rim_row(facts, g, width) for g in range(4)]


def write_slots(refs, messages):
    for g, ref in enumerate(refs):
        ref[...] = messages[:, g * SLOT : (g + 1) * SLOT].astype(BF)


def read_slots(refs):
    return jnp.concatenate([r[...] for r in refs], axis=1)


def columns_mask():
    lane = lax.broadcasted_iota(jnp.int32, (1, INNER), 1)
    return lax.rem(lane, PITCH) < S


def taps(reach):
    return [(a - 1) * PITCH * reach + (b - 1) * reach for a in range(3) for b in range(3)]


def gelu_parts(x):
    k = math.sqrt(2.0 / math.pi)
    sq = x * x
    t = jnp.tanh(k * x * (1.0 + 0.044715 * sq))
    half = 0.5 * (1.0 + t)
    slope = half + 0.5 * x * (1.0 - t * t) * (k * (1.0 + 3.0 * 0.044715 * sq))
    return x * half, slope


def gather_taps(col, wide, reach, sign, start, count):
    for n, off in enumerate(taps(reach)):
        lo = BASE + start + sign * off
        col[C * n : C * (n + 1), :] = wide[:, lo : lo + count]


def up_matrix():
    m = lax.broadcasted_iota(jnp.int32, (1, 256), 1)
    place = lax.broadcasted_iota(jnp.int32, (INNER, 256), 0)
    return jnp.where(place == 72 * (m >> 4) + 2 * (m & 15), 1.0, 0.0).astype(BF)


def send_inputs_body(facts, x, *slots):
    hot = pick(sources(facts, 1, S, 0), 0, S * S)
    write_slots(slots, mm(x[...], hot))


def prepare_body(x, cot, down_t, spread, upstream, grad_two, wide, col):
    spread[...] = jnp.zeros_like(spread)
    for y in range(S):
        spread[:, BASE + PITCH * y : BASE + PITCH * y + S] = x[:, S * y : S * y + S]
    wide[...] = jnp.zeros_like(wide)
    wide[:, BASE : BASE + INNER] = nt(cot[...], up_matrix()).astype(BF)
    for n in range(4):
        lo = BASE - (n // 2) * PITCH - n % 2
        col[C * n : C * (n + 1), :] = wide[:, lo : lo + INNER]
    upstream[...] = wide[:, BASE : BASE + INNER]
    grad_two[...] = mm(down_t[...], col[...])


def first_body(facts, spread, r0, r1, r2, r3, w, ext, hidden, slope, m0, m1, m2, m3, wide, col):
    halo = nt(read_slots((r0, r1, r2, r3)), pick(rims(facts, 1), 0, FULL)).astype(BF)
    full = spread[...] + halo
    ext[...] = full
    wide[...] = jnp.zeros_like(wide)
    wide[:, BASE : BASE + FULL] = full
    gather_taps(col, wide, 1, 1, BASE, INNER)
    value, grad = gelu_parts(mm(w[...], col[...]))
    value = jnp.where(columns_mask(), value, 0.0).astype(BF)
    hidden[...] = value
    slope[...] = grad
    write_slots((m0, m1, m2, m3), mm(value, pick(sources(facts, 2), BASE, INNER)))


def second_body(
    facts, hidden, r0, r1, r2, r3, w, wt, grad_two,
    ext, hidden_two, delta, grad_mid, m0, m1, m2, m3, wide, col, col_full,
):
    rim = pick(rims(facts, 2), 0, FULL)
    halo = nt(read_slots((r0, r1, r2, r3)), rim).astype(BF)
    wide[...] = jnp.zeros_like(wide)
    wide[:, BASE : BASE + FULL] = halo
    wide[:, 2 * BASE : 2 * BASE + INNER] = halo[:, BASE : BASE + INNER] + hidden[...]
    ext[...] = wide[:, BASE : BASE + FULL]
    gather_taps(col, wide, 2, 1, BASE, INNER)
    value, grad = gelu_parts(mm(w[...], col[...]))
    hidden_two[...] = value.astype(BF)
    back = jnp.where(columns_mask(), grad * grad_two[...], 0.0).astype(BF)
    delta[...] = back
    wide[...] = jnp.zeros_like(wide)
    wide[:, 2 * BASE : 2 * BASE + INNER] = back
    gather_taps(col_full, wide, 2, -1, 0, FULL)
    pad = mm(wt[...], col_full[...])
    grad_mid[...] = pad[:, BASE : BASE + INNER]
    write_slots((m0, m1, m2, m3), mm(pad.astype(BF), rim))


def second_sums_body(scale, ext, hidden_two, delta, upstream, down, encoded, grad, grad_down, wide, col):
    wide[...] = jnp.zeros_like(wide)
    wide[:, BASE : BASE + FULL] = ext[...]
    gather_taps(col, wide, 2, 1, BASE, INNER)
    grad[...] = nt(delta[...], col[...]) * scale
    wide[:, 2 * BASE : 2 * BASE + INNER] = hidden_two[...]
    for n in range(4):
        lo = 2 * BASE + (n // 2) * PITCH + n % 2
        col[C * n : C * (n + 1), :] = wide[:, lo : lo + INNER]
    four = col[: 4 * C, :]
    grad_down[...] = nt(upstream[...], four) * scale
    encoded[...] = mm(mm(down[...], four).astype(BF), up_matrix()).astype(BF)


def third_body(scale, facts, grad_mid, r0, r1, r2, r3, slope, ext, delta, grad, wide, col):
    back = nt(read_slots((r0, r1, r2, r3)), pick(sources(facts, 2), BASE, INNER))
    back = (grad_mid[...] + back) * slope[...]
    back = jnp.where(columns_mask(), back, 0.0).astype(BF)
    delta[...] = back
    wide[...] = jnp.zeros_like(wide)
    wide[:, BASE : BASE + FULL] = ext[...]
    gather_taps(col, wide, 1, 1, BASE, INNER)
    grad[...] = nt(back, col[...]) * scale


def fourth_body(facts, delta, wt, grad, m0, m1, m2, m3, wide, col_full):
    wide[...] = jnp.zeros_like(wide)
    wide[:, 2 * BASE : 2 * BASE + INNER] = delta[...]
    gather_taps(col_full, wide, 1, -1, 0, FULL)
    pad = mm(wt[...], col_full[...])
    grad[...] = pad[:, BASE : BASE + INNER]
    write_slots((m0, m1, m2, m3), mm(pad.astype(BF), pick(rims(facts, 1), 0, FULL)))


def last_body(facts, grad, r0, r1, r2, r3, o):
    back = nt(read_slots((r0, r1, r2, r3)), pick(sources(facts, 1), BASE, INNER))
    back = (grad[...] + back).astype(BF)
    for y in range(S):
        o[:, S * y : S * y + S] = back[:, PITCH * y : PITCH * y + S]


def swap(value, step, parity):
    count = lax.axis_size("tile")
    pairs = []
    for t in range(count):
        if (t // step) % 2 == parity:
            u = (t + step) % count
            pairs += [(t, u), (u, t)]
    return lax.ppermute(value, "tile", pairs)


def lane():
    return lax.broadcasted_iota(jnp.int32, (C, SLOT), 1)


def exchange(m):
    r3 = swap(m[3], 1, 1)
    r2 = swap(m[2], 1, 0)
    corners = jnp.where(((lane() >> 2) & 1) == 0, r2, r3)
    r1 = swap(jnp.where(lane() < CORNER, m[1], corners), ROW_TILES, 1)
    r0 = swap(jnp.where(lane() < CORNER, m[0], corners), ROW_TILES, 0)
    return r0, r1, r2, r3


def exchange_back(m):
    r1 = swap(m[1], ROW_TILES, 1)
    r0 = swap(m[0], ROW_TILES, 0)
    corners = r0 + r1
    r3 = swap(jnp.where(lane() < CORNER, m[3], corners), 1, 1)
    r2 = swap(jnp.where(lane() < CORNER, m[2], corners), 1, 0)
    return r0, r1, r2, r3


def add_up(values):
    count = lax.axis_size("tile")
    core = lax.axis_index("tile") % 2
    half = values.shape[0] // 2
    low, high = values[:half], values[half:]

    def across(v, axis, bit, n):
        return lax.ppermute(v, axis, [(i, i ^ bit) for i in range(n)])

    got = across(jnp.where(core == 0, high, low), "tile", 1, count)
    part = jnp.where(core == 0, low, high) + got
    for axis, bit in [("member", 1)] + [("tile", 2**k) for k in range(4, 7)] + [("tile", 2**k) for k in range(1, 4)]:
        part = part.astype(BF)
        got = across(part, axis, bit, lax.axis_size(axis))
        part = part.astype(F32) + got.astype(F32)
    other = across(part, "tile", 1, count)
    first, then = jnp.where(core == 0, part, other), jnp.where(core == 0, other, part)
    return jnp.concatenate([first, then], axis=0)


def per_device(inputs, cotangent, seam_codes, conv_one, conv_two, down_weight):
    x, cot = inputs[0, 0], cotangent[0, 0]
    tile = lax.axis_index("tile").astype(jnp.int32)
    down_row = (tile // ROW_TILES) % 2 == 0
    even = tile % 2 == 0
    sides = jnp.stack(
        [jnp.where(down_row, 2, 0), jnp.where(down_row, 0, 2), jnp.where(even, 1, 3), jnp.where(even, 3, 1)]
    ).astype(jnp.int32)
    facts = jnp.concatenate([sides, seam_codes[0][sides]]).reshape(1, 8)
    count = lax.axis_size("tile") * lax.axis_size("member")
    scale = 1.0 / math.sqrt(count * S * S)

    def flip(w, n):
        return jnp.transpose(w.reshape(C, n, C), (2, 1, 0)).reshape(C, n * C)

    one_t, two_t, down_t = flip(conv_one, 9), flip(conv_two, 9), flip(down_weight, 4)
    slots = [out((C, SLOT), BF)] * 4
    wide, col = pltpu.VMEM((C, WIDE), BF), pltpu.VMEM((9 * C, INNER), BF)
    col_full = pltpu.VMEM((9 * C, FULL), BF)
    dense = 2 * C * 9 * C * INNER

    sent = call(send_inputs_body, slots, [], [facts, x], 2 * C * 1024 * 512, "send_inputs")
    spread, upstream, grad_two = call(
        prepare_body,
        [out((C, FULL), BF), out((C, INNER), BF), out((C, INNER), F32)],
        [wide, pltpu.VMEM((4 * C, INNER), BF)],
        [x, cot, down_t],
        dense,
        "prepare",
    )
    got = exchange(sent)
    ext, hidden, slope, *sent = call(
        first_body,
        [out((C, FULL), BF), out((C, INNER), BF), out((C, INNER), F32)] + slots,
        [wide, col],
        [facts, spread, *got, conv_one],
        2 * dense,
        "first",
    )
    got = exchange(sent)
    ext_two, hidden_two, delta_two, grad_mid, *sent = call(
        second_body,
        [out((C, FULL), BF), out((C, INNER), BF), out((C, INNER), BF), out((C, INNER), F32)] + slots,
        [wide, col, col_full],
        [facts, hidden, *got, conv_two, two_t, grad_two],
        3 * dense,
        "second",
    )
    got = exchange_back(sent)
    encoded, sum_two, sum_down = call(
        lambda *refs: second_sums_body(scale, *refs),
        [out((C, 256), BF), out((C, 9 * C), F32), out((C, 4 * C), F32)],
        [wide, col],
        [ext_two, hidden_two, delta_two, upstream, down_weight],
        2 * dense,
        "second_sums",
    )
    delta_one, sum_one = call(
        lambda *refs: third_body(scale, *refs),
        [out((C, INNER), BF), out((C, 9 * C), F32)],
        [wide, col],
        [facts, grad_mid, *got, slope, ext],
        2 * dense,
        "third",
    )
    grad_in, *sent = call(
        fourth_body,
        [out((C, INNER), F32)] + slots,
        [wide, col_full],
        [facts, delta_one, one_t],
        2 * dense,
        "fourth",
    )
    got = exchange_back(sent)
    (input_grad,) = call(
        last_body, [out((C, S * S), BF)], [], [facts, grad_in, *got], dense, "last"
    )
    total = add_up(jnp.concatenate([sum_one, sum_two, sum_down], axis=1))
    return (
        encoded.reshape(1, 1, C, 256),
        input_grad.reshape(1, 1, C, S * S),
        total[:, : 9 * C],
        total[:, 9 * C : 18 * C],
        total[:, 18 * C :],
    )


def solution(mesh):
    split = P("member", "tile", None, None)
    return jax.shard_map(
        per_device,
        mesh=mesh,
        in_specs=(split, split, P("tile", None), P(), P(), P()),
        out_specs=(split, split, P(), P(), P()),
        check_vma=False,
    )
```

```python
import math

import jax
import jax.numpy as jnp
from jax import lax
from jax.experimental import pallas as pl
from jax.experimental.pallas import tpu as pltpu
from jax.sharding import Mesh, PartitionSpec as P

S = 32
C = 64
ROW_TILES = 8
PITCH = 36
BASE = 128
INNER = S * PITCH
FULL = INNER + 2 * BASE
WIDE = FULL + 2 * BASE
SLOT = 128
PACKED = 12 * C
TILE = ("x", "y", "z", "core")
MEMBER = ("member",)
NEAR = ("z", "core")
FAR = ("x", "y", "member")
CODES = S * S + 256
LOAD = CODES + SLOT
CORNER = 64
BF = jnp.bfloat16
F32 = jnp.float32


def call(body, outs, scratch, args, flops, name):
    specs = [
        pl.BlockSpec(memory_space=pltpu.SMEM if a.shape == (1, 4) else pltpu.VMEM) for a in args
    ]
    moved = sum(math.prod(o.shape) * o.dtype.itemsize for o in list(outs) + list(args))
    return pl.pallas_call(
        body,
        out_shape=outs,
        in_specs=specs,
        out_specs=[pl.BlockSpec(memory_space=pltpu.VMEM)] * len(outs),
        scratch_shapes=scratch,
        compiler_params=pltpu.CompilerParams(vmem_limit_bytes=24 * 2**20),
        cost_estimate=pl.CostEstimate(flops=flops, bytes_accessed=moved, transcendentals=0),
        name=name,
    )(*args)


def out(shape, dtype):
    return jax.ShapeDtypeStruct(shape, dtype)


def nt(a, b):
    return lax.dot_general(a, b, (((1,), (1,)), ((), ())), preferred_element_type=F32)


def mm(a, b):
    return jnp.dot(a, b, preferred_element_type=F32)


def lanes_of():
    lane = lax.broadcasted_iota(jnp.int32, (1, SLOT), 1)
    part = lane - CORNER
    return lane, lane >> 5, lane & 31, part, part >> 2, part & 3


def corner_offsets(j, width):
    if width == 2:
        return j >> 1, j & 1, j >= 0
    return 0 * j, 0 * j, j == 0


def source_row(facts, group, width, pitch, base):
    lane, depth, along, part, kind, j = lanes_of()
    side, code = facts[group : group + 1, :], facts[4 + group : 5 + group, :]
    edge = (side - code + 4) & 3
    along = jnp.where((code & 1) == 1, 31 - along, along)
    near = jnp.where((edge == 1) | (edge == 2), 31 - depth, depth)
    rows = (edge & 1) == 0
    y = jnp.where(rows, near, along)
    x = jnp.where(rows, along, near)
    valid = lane < S * width
    if group >= 2:
        u, v, there = corner_offsets(j, width)
        mine = (part >= 0) & (kind < 4) & ((kind & 1) == group - 2) & there
        cy = jnp.where(kind >= 2, S - width + u, u)
        cx = jnp.where(side == 1, S - width + v, v)
        y = jnp.where(mine, cy, y)
        x = jnp.where(mine, cx, x)
        valid = valid | mine
    return jnp.where(valid, base + pitch * y + x, -1)


def rim_row(facts, group, width):
    lane, depth, along, part, kind, j = lanes_of()
    side, second = facts[group : group + 1, :], facts[2:3, :]
    beyond = jnp.where((side == 0) | (side == 3), -1 - depth, S + depth)
    rows = (side & 1) == 0
    y = jnp.where(rows, beyond, along)
    x = jnp.where(rows, along, beyond)
    valid = lane < S * width
    if group < 2:
        u, v, there = corner_offsets(j, width)
        south = jnp.where(side == 0, 1, 0)
        mine = (part >= 0) & (kind < 4) & ((kind >> 1) == south) & there
        east = jnp.where((kind & 1) == 0, second, 4 - second) == 1
        cy = jnp.where(side == 0, u - width, S + u)
        cx = jnp.where(east, S + v, v - width)
        y = jnp.where(mine, cy, y)
        x = jnp.where(mine, cx, x)
        valid = valid | mine
    return jnp.where(valid, BASE + PITCH * y + x, -1)


def pick(rows, start, count):
    row = jnp.concatenate(rows, axis=1)
    place = start + lax.broadcasted_iota(jnp.int32, (count, row.shape[1]), 0)
    return jnp.where(place == row, 1.0, 0.0).astype(BF)


def sources(facts, width, pitch=PITCH, base=BASE):
    return [source_row(facts, g, width, pitch, base) for g in range(4)]


def rims(facts, width):
    return [rim_row(facts, g, width) for g in range(4)]


def write_slots(refs, messages):
    for g, ref in enumerate(refs):
        ref[...] = messages[:, g * SLOT : (g + 1) * SLOT].astype(BF)


def read_slots(refs):
    return jnp.concatenate([r[...] for r in refs], axis=1)


def columns_mask():
    lane = lax.broadcasted_iota(jnp.int32, (1, INNER), 1)
    return lax.rem(lane, PITCH) < S


def taps(reach):
    return [(a - 1) * PITCH * reach + (b - 1) * reach for a in range(3) for b in range(3)]


def gelu_parts(x):
    k = math.sqrt(2.0 / math.pi)
    sq = x * x
    t = jnp.tanh(k * x * (1.0 + 0.044715 * sq))
    half = 0.5 * (1.0 + t)
    slope = half + 0.5 * x * (1.0 - t * t) * (k * (1.0 + 3.0 * 0.044715 * sq))
    return x * half, slope


def gather_taps(col, wide, reach, sign, start, count):
    for n, off in enumerate(taps(reach)):
        lo = BASE + start + sign * off
        col[C * n : C * (n + 1), :] = wide[:, lo : lo + count]


def up_matrix():
    m = lax.broadcasted_iota(jnp.int32, (1, 256), 1)
    place = lax.broadcasted_iota(jnp.int32, (INNER, 256), 0)
    return jnp.where(place == 72 * (m >> 4) + 2 * (m & 15), 1.0, 0.0).astype(BF)


def load_body(codes, x, cot, load):
    load[:, : S * S] = x[...]
    load[:, S * S : CODES] = cot[...]
    row = lax.broadcasted_iota(jnp.int32, (C, SLOT), 0)
    value = jnp.where(row == 0, codes[0, 0], jnp.where(row == 1, codes[0, 1], jnp.where(row == 2, codes[0, 2], codes[0, 3])))
    load[:, CODES:] = value.astype(F32).astype(BF)


def send_inputs_body(load, facts, *slots):
    codes = load[:16, CODES:].astype(F32).astype(jnp.int32)
    row, column = lax.axis_index("core"), lax.axis_index("z") & 1
    sides = [2 - 2 * row, 2 * row, 1 + 2 * column, 3 - 2 * column]
    for g, side in enumerate(sides):
        code = jnp.where(side == 2, codes[2:3, :], codes[3:4, :])
        code = jnp.where(side == 1, codes[1:2, :], code)
        code = jnp.where(side == 0, codes[0:1, :], code)
        facts[g : g + 1, :] = jnp.full((1, SLOT), side, jnp.int32)
        facts[4 + g : 5 + g, :] = code
    hot = pick(sources(facts, 1, S, 0), 0, S * S)
    write_slots(slots, mm(load[:, : S * S], hot))


def transpose_taps(src, dst, count):
    for n in range(count):
        block = src[:, C * n : C * (n + 1)].astype(F32)
        dst[:, C * n : C * (n + 1)] = jnp.transpose(block).astype(BF)


def prepare_body(load, down, one, two, spread, upstream, grad_two, one_t, two_t, wide, col, down_t):
    transpose_taps(one, one_t, 9)
    transpose_taps(two, two_t, 9)
    transpose_taps(down, down_t, 4)
    spread[...] = jnp.zeros_like(spread)
    for y in range(S):
        spread[:, BASE + PITCH * y : BASE + PITCH * y + S] = load[:, S * y : S * y + S]
    wide[...] = jnp.zeros_like(wide)
    wide[:, BASE : BASE + INNER] = nt(load[:, S * S : CODES], up_matrix()).astype(BF)
    for n in range(4):
        lo = BASE - (n // 2) * PITCH - n % 2
        col[C * n : C * (n + 1), :] = wide[:, lo : lo + INNER]
    upstream[...] = wide[:, BASE : BASE + INNER]
    grad_two[...] = mm(down_t[...], col[...])


def first_body(facts, spread, r0, r1, r2, r3, w, ext, hidden, slope, m0, m1, m2, m3, wide, col):
    halo = nt(read_slots((r0, r1, r2, r3)), pick(rims(facts, 1), 0, FULL)).astype(BF)
    full = spread[...] + halo
    ext[...] = full
    wide[...] = jnp.zeros_like(wide)
    wide[:, BASE : BASE + FULL] = full
    gather_taps(col, wide, 1, 1, BASE, INNER)
    value, grad = gelu_parts(mm(w[...], col[...]))
    value = jnp.where(columns_mask(), value, 0.0).astype(BF)
    hidden[...] = value
    slope[...] = grad
    write_slots((m0, m1, m2, m3), mm(value, pick(sources(facts, 2), BASE, INNER)))


def second_body(
    facts, hidden, r0, r1, r2, r3, w, wt, grad_two,
    ext, hidden_two, delta, grad_mid, m0, m1, m2, m3, wide, col, col_full,
):
    rim = pick(rims(facts, 2), 0, FULL)
    halo = nt(read_slots((r0, r1, r2, r3)), rim).astype(BF)
    wide[...] = jnp.zeros_like(wide)
    wide[:, BASE : BASE + FULL] = halo
    wide[:, 2 * BASE : 2 * BASE + INNER] = halo[:, BASE : BASE + INNER] + hidden[...]
    ext[...] = wide[:, BASE : BASE + FULL]
    gather_taps(col, wide, 2, 1, BASE, INNER)
    value, grad = gelu_parts(mm(w[...], col[...]))
    hidden_two[...] = value.astype(BF)
    back = jnp.where(columns_mask(), grad * grad_two[...], 0.0).astype(BF)
    delta[...] = back
    wide[...] = jnp.zeros_like(wide)
    wide[:, 2 * BASE : 2 * BASE + INNER] = back
    gather_taps(col_full, wide, 2, -1, 0, FULL)
    pad = mm(wt[...], col_full[...])
    grad_mid[...] = pad[:, BASE : BASE + INNER]
    write_slots((m0, m1, m2, m3), mm(pad.astype(BF), rim))


def second_sums_body(scale, ext, hidden_two, delta, upstream, down, encoded, grad, grad_down, wide, col):
    wide[...] = jnp.zeros_like(wide)
    wide[:, BASE : BASE + FULL] = ext[...]
    gather_taps(col, wide, 2, 1, BASE, INNER)
    grad[...] = nt(delta[...], col[...]) * scale
    wide[:, 2 * BASE : 2 * BASE + INNER] = hidden_two[...]
    for n in range(4):
        lo = 2 * BASE + (n // 2) * PITCH + n % 2
        col[C * n : C * (n + 1), :] = wide[:, lo : lo + INNER]
    four = col[: 4 * C, :]
    grad_down[...] = nt(upstream[...], four) * scale
    encoded[...] = mm(mm(down[...], four).astype(BF), up_matrix()).astype(BF)


def third_body(scale, facts, grad_mid, r0, r1, r2, r3, slope, ext, sum_two, sum_down, delta, packed, wide, col):
    back = nt(read_slots((r0, r1, r2, r3)), pick(sources(facts, 2), BASE, INNER))
    back = (grad_mid[...] + back) * slope[...]
    back = jnp.where(columns_mask(), back, 0.0).astype(BF)
    delta[...] = back
    wide[...] = jnp.zeros_like(wide)
    wide[:, BASE : BASE + FULL] = ext[...]
    gather_taps(col, wide, 1, 1, BASE, INNER)
    sums = [nt(back, col[...]) * scale, sum_two[...], sum_down[...], jnp.zeros((C, SLOT), F32)]
    sums = jnp.concatenate(sums, axis=1)
    for n in range(PACKED // C):
        packed[C * n : C * (n + 1), :] = sums[:, SLOT * n : SLOT * (n + 1)].astype(BF)


def unpack_body(packed, one, two, down):
    sums = [packed[C * n : C * (n + 1), :].astype(F32) for n in range(PACKED // C - 1)]
    sums = jnp.concatenate(sums, axis=1)
    one[...] = sums[:, : 9 * C]
    two[...] = sums[:, 9 * C : 18 * C]
    down[...] = sums[:, 18 * C :]


def fourth_body(facts, delta, wt, grad, m0, m1, m2, m3, wide, col_full):
    wide[...] = jnp.zeros_like(wide)
    wide[:, 2 * BASE : 2 * BASE + INNER] = delta[...]
    gather_taps(col_full, wide, 1, -1, 0, FULL)
    pad = mm(wt[...], col_full[...])
    grad[...] = pad[:, BASE : BASE + INNER]
    write_slots((m0, m1, m2, m3), mm(pad.astype(BF), pick(rims(facts, 1), 0, FULL)))


def last_body(facts, grad, r0, r1, r2, r3, encoded, o):
    o[:, S * S :] = encoded[...]
    back = nt(read_slots((r0, r1, r2, r3)), pick(sources(facts, 1), BASE, INNER))
    back = (grad[...] + back).astype(BF)
    for y in range(S):
        o[:, S * y : S * y + S] = back[:, PITCH * y : PITCH * y + S]


def home(t):
    row, column = t // ROW_TILES, t % ROW_TILES
    x = row // 4
    y = (row // 2 % 2) ^ (x % 2)
    return ((x * 2 + y) * 8 + column) * 2 + row % 2


def move(value, pairs):
    return lax.ppermute(value, TILE, pairs)


def swap(value, step, parity):
    count = lax.axis_size(TILE)
    pairs = []
    for t in range(count):
        if (t // step) % 2 == parity:
            here, there = home(t), home((t + step) % count)
            pairs += [(here, there), (there, here)]
    return move(value, pairs)


def lane():
    return lax.broadcasted_iota(jnp.int32, (C, SLOT), 1)


def exchange(m):
    r3 = swap(m[3], 1, 1)
    r2 = swap(m[2], 1, 0)
    corners = jnp.where(((lane() >> 2) & 1) == 0, r2, r3)
    r1 = swap(jnp.where(lane() < CORNER, m[1], corners), ROW_TILES, 1)
    r0 = swap(jnp.where(lane() < CORNER, m[0], corners), ROW_TILES, 0)
    return r0, r1, r2, r3


def exchange_back(m):
    r1 = swap(m[1], ROW_TILES, 1)
    r0 = swap(m[0], ROW_TILES, 0)
    corners = r0 + r1
    r3 = swap(jnp.where(lane() < CORNER, m[3], corners), 1, 1)
    r2 = swap(jnp.where(lane() < CORNER, m[2], corners), 1, 0)
    return r0, r1, r2, r3


def add_up(packed):
    share = PACKED // lax.axis_size(NEAR)

    def trade(v, axes):
        return lax.all_to_all(v, axes, 0, 0, tiled=True)

    def total(v):
        return jnp.sum(v.astype(F32), axis=0).astype(BF)

    def everyone(v, axes):
        return jnp.broadcast_to(v[None], (lax.axis_size(axes),) + v.shape)

    part = total(trade(packed.reshape(-1, share, SLOT), NEAR))
    part = total(trade(everyone(part, FAR), FAR))
    return trade(everyone(part, NEAR), NEAR).reshape(PACKED, SLOT)


def per_device(inputs, cotangent, seam_codes, conv_one, conv_two, down_weight):
    x, cot = inputs[0, 0], cotangent[0, 0]
    assert lax.axis_size(TILE) == 128
    scale = 1.0 / math.sqrt(lax.axis_size(TILE + MEMBER) * S * S)

    slots = [out((C, SLOT), BF)] * 4
    wide, col = pltpu.VMEM((C, WIDE), BF), pltpu.VMEM((9 * C, INNER), BF)
    col_full = pltpu.VMEM((9 * C, FULL), BF)
    dense = 2 * C * 9 * C * INNER

    (load,) = call(load_body, [out((C, LOAD), BF)], [], [seam_codes, x, cot], C * LOAD, "load")
    load = move(load, [(t, home(t)) for t in range(128)])
    facts, *sent = call(
        send_inputs_body, [out((8, SLOT), jnp.int32)] + slots, [], [load], 2 * C * 1024 * 512, "send_inputs"
    )
    spread, upstream, grad_two, one_t, two_t = call(
        prepare_body,
        [out((C, FULL), BF), out((C, INNER), BF), out((C, INNER), F32)] + [out((C, 9 * C), BF)] * 2,
        [wide, pltpu.VMEM((4 * C, INNER), BF), pltpu.VMEM((C, 4 * C), BF)],
        [load, down_weight, conv_one, conv_two],
        dense,
        "prepare",
    )
    got = exchange(sent)
    ext, hidden, slope, *sent = call(
        first_body,
        [out((C, FULL), BF), out((C, INNER), BF), out((C, INNER), F32)] + slots,
        [wide, col],
        [facts, spread, *got, conv_one],
        2 * dense,
        "first",
    )
    got = exchange(sent)
    ext_two, hidden_two, delta_two, grad_mid, *sent = call(
        second_body,
        [out((C, FULL), BF), out((C, INNER), BF), out((C, INNER), BF), out((C, INNER), F32)] + slots,
        [wide, col, col_full],
        [facts, hidden, *got, conv_two, two_t, grad_two],
        3 * dense,
        "second",
    )
    got = exchange_back(sent)
    encoded, sum_two, sum_down = call(
        lambda *refs: second_sums_body(scale, *refs),
        [out((C, 256), BF), out((C, 9 * C), F32), out((C, 4 * C), F32)],
        [wide, col],
        [ext_two, hidden_two, delta_two, upstream, down_weight],
        2 * dense,
        "second_sums",
    )
    delta_one, packed = call(
        lambda *refs: third_body(scale, *refs),
        [out((C, INNER), BF), out((PACKED, SLOT), BF)],
        [wide, col],
        [facts, grad_mid, *got, slope, ext, sum_two, sum_down],
        2 * dense,
        "third",
    )
    grad_in, *sent = call(
        fourth_body,
        [out((C, INNER), F32)] + slots,
        [wide, col_full],
        [facts, delta_one, one_t],
        2 * dense,
        "fourth",
    )
    got = exchange_back(sent)
    (results,) = call(
        last_body, [out((C, CODES), BF)], [], [facts, grad_in, *got, encoded], dense, "last"
    )
    results = move(results, [(home(t), t) for t in range(128)])
    sums = call(
        unpack_body,
        [out((C, 9 * C), F32), out((C, 9 * C), F32), out((C, 4 * C), F32)],
        [],
        [add_up(packed)],
        C * C,
        "unpack",
    )
    return (
        results[:, S * S :].reshape(1, 1, C, 256),
        results[:, : S * S].reshape(1, 1, C, S * S),
        *sums,
    )


def solution(mesh):
    axes = Mesh(mesh.devices.reshape(4, 2, 8, 2, 2), TILE + MEMBER)
    split = P(MEMBER, TILE, None, None)
    return jax.shard_map(
        per_device,
        mesh=axes,
        in_specs=(split, split, P(TILE, None), P(), P(), P()),
        out_specs=(split, split, P(), P(), P()),
        check_vma=False,
    )
```

```python
import math

import jax
import jax.numpy as jnp
from jax import lax
from jax.experimental import pallas as pl
from jax.experimental.pallas import tpu as pltpu
from jax.sharding import Mesh, PartitionSpec as P

S = 32
C = 64
ROW_TILES = 8
PITCH = 36
BASE = 128
INNER = S * PITCH
FULL = INNER + 2 * BASE
WIDE = FULL + 2 * BASE
SLOT = 128
PACKED = 12 * C
TILE = ("x", "y", "z", "core")
MEMBER = ("member",)
NEAR = ("z", "core")
FAR = ("x", "y", "member")
LOAD = S * S + 256
RING = ((1, 0), (0, 0), (0, 1), (1, 1), (2, 1), (3, 1), (3, 0), (2, 0))
CORNER = 64
BF = jnp.bfloat16
F32 = jnp.float32


def call(body, outs, scratch, args, flops, name, space=pltpu.VMEM, limit=24):
    specs = [pl.BlockSpec(memory_space=space) for a in args]
    moved = sum(math.prod(o.shape) * o.dtype.itemsize for o in list(outs) + list(args))
    return pl.pallas_call(
        body,
        out_shape=outs,
        in_specs=specs,
        out_specs=[pl.BlockSpec(memory_space=pltpu.VMEM)] * len(outs),
        scratch_shapes=scratch,
        compiler_params=pltpu.CompilerParams(vmem_limit_bytes=limit * 2**20),
        cost_estimate=pl.CostEstimate(flops=flops, bytes_accessed=moved, transcendentals=0),
        name=name,
    )(*args)


def out(shape, dtype):
    return jax.ShapeDtypeStruct(shape, dtype)


def nt(a, b):
    return lax.dot_general(a, b, (((1,), (1,)), ((), ())), preferred_element_type=F32)


def mm(a, b):
    return jnp.dot(a, b, preferred_element_type=F32)


def lanes_of():
    lane = lax.broadcasted_iota(jnp.int32, (1, SLOT), 1)
    part = lane - CORNER
    return lane, lane >> 5, lane & 31, part, part >> 2, part & 3


def corner_offsets(j, width):
    if width == 2:
        return j >> 1, j & 1, j >= 0
    return 0 * j, 0 * j, j == 0


def source_row(facts, group, width, pitch, base):
    lane, depth, along, part, kind, j = lanes_of()
    side, code = facts[group : group + 1, :], facts[4 + group : 5 + group, :]
    edge = (side - code + 4) & 3
    along = jnp.where((code & 1) == 1, 31 - along, along)
    near = jnp.where((edge == 1) | (edge == 2), 31 - depth, depth)
    rows = (edge & 1) == 0
    y = jnp.where(rows, near, along)
    x = jnp.where(rows, along, near)
    valid = lane < S * width
    if group >= 2:
        u, v, there = corner_offsets(j, width)
        mine = (part >= 0) & (kind < 4) & ((kind & 1) == group - 2) & there
        cy = jnp.where(kind >= 2, S - width + u, u)
        cx = jnp.where(side == 1, S - width + v, v)
        y = jnp.where(mine, cy, y)
        x = jnp.where(mine, cx, x)
        valid = valid | mine
    return jnp.where(valid, base + pitch * y + x, -1)


def rim_row(facts, group, width):
    lane, depth, along, part, kind, j = lanes_of()
    side, second = facts[group : group + 1, :], facts[2:3, :]
    beyond = jnp.where((side == 0) | (side == 3), -1 - depth, S + depth)
    rows = (side & 1) == 0
    y = jnp.where(rows, beyond, along)
    x = jnp.where(rows, along, beyond)
    valid = lane < S * width
    if group < 2:
        u, v, there = corner_offsets(j, width)
        south = jnp.where(side == 0, 1, 0)
        mine = (part >= 0) & (kind < 4) & ((kind >> 1) == south) & there
        east = jnp.where((kind & 1) == 0, second, 4 - second) == 1
        cy = jnp.where(side == 0, u - width, S + u)
        cx = jnp.where(east, S + v, v - width)
        y = jnp.where(mine, cy, y)
        x = jnp.where(mine, cx, x)
        valid = valid | mine
    return jnp.where(valid, BASE + PITCH * y + x, -1)


def pick(rows, start, count):
    row = jnp.concatenate(rows, axis=1)
    place = start + lax.broadcasted_iota(jnp.int32, (count, row.shape[1]), 0)
    return jnp.where(place == row, 1.0, 0.0).astype(BF)


def sources(facts, width, pitch=PITCH, base=BASE):
    return [source_row(facts, g, width, pitch, base) for g in range(4)]


def rims(facts, width):
    return [rim_row(facts, g, width) for g in range(4)]


def write_slots(refs, messages):
    for g, ref in zip((3, 2, 1, 0), refs, strict=True):
        ref[...] = messages[:, g * SLOT : (g + 1) * SLOT].astype(BF)


def read_slots(refs):
    return jnp.concatenate([r[...] for r in refs], axis=1)


def columns_mask():
    lane = lax.broadcasted_iota(jnp.int32, (1, INNER), 1)
    return lax.rem(lane, PITCH) < S


def taps(reach):
    return [(a - 1) * PITCH * reach + (b - 1) * reach for a in range(3) for b in range(3)]


def gelu_parts(x):
    k = math.sqrt(2.0 / math.pi)
    sq = x * x
    t = jnp.tanh(k * x * (1.0 + 0.044715 * sq))
    half = 0.5 * (1.0 + t)
    slope = half + 0.5 * x * (1.0 - t * t) * (k * (1.0 + 3.0 * 0.044715 * sq))
    return x * half, slope


def gather_taps(col, wide, reach, sign, start, count):
    for n, off in enumerate(taps(reach)):
        lo = BASE + start + sign * off
        col[C * n : C * (n + 1), :] = wide[:, lo : lo + count]


def up_matrix():
    m = lax.broadcasted_iota(jnp.int32, (1, 256), 1)
    place = lax.broadcasted_iota(jnp.int32, (INNER, 256), 0)
    return jnp.where(place == 72 * (m >> 4) + 2 * (m & 15), 1.0, 0.0).astype(BF)


def load_body(codes_hbm, x_hbm, cot_hbm, one_hbm, two_hbm, down_hbm, edges, load, one, two, down, codes, sems):
    later = [
        pltpu.make_async_copy(one_hbm, one, sems.at[3]),
        pltpu.make_async_copy(two_hbm, two, sems.at[4]),
        pltpu.make_async_copy(down_hbm, down, sems.at[5]),
    ]
    copies = [
        pltpu.make_async_copy(codes_hbm, codes, sems.at[0]),
        pltpu.make_async_copy(x_hbm, load.at[:, pl.ds(0, S * S)], sems.at[1]),
        pltpu.make_async_copy(cot_hbm, load.at[:, pl.ds(S * S, 256)], sems.at[2]),
    ]
    for copy in copies + later:
        copy.start()
    lane, edge, along = lanes_of()[:3]
    y = jnp.where((edge & 1) == 0, jnp.where(edge == 0, 0, S - 1), along)
    x = jnp.where((edge & 1) == 0, along, jnp.where(edge == 1, S - 1, 0))
    hot = pick([S * y + x], 0, S * S)
    for copy in copies:
        copy.wait()
    edges[:, :SLOT] = mm(load[:, : S * S], hot).astype(BF)
    row = lax.broadcasted_iota(jnp.int32, (C, SLOT), 0)
    value = jnp.where(row == 0, codes[0, 0], jnp.where(row == 1, codes[0, 1], jnp.where(row == 2, codes[0, 2], codes[0, 3])))
    edges[:, SLOT:] = value.astype(F32).astype(BF)
    for copy in later:
        copy.wait()


def edge_row(facts, group):
    lane, _, along, part, kind, j = lanes_of()
    side, code = facts[group : group + 1, :], facts[4 + group : 5 + group, :]
    along = jnp.where((code & 1) == 1, 31 - along, along)
    place = S * ((side - code + 4) & 3) + along
    valid = lane < S
    if group >= 2:
        mine = (part >= 0) & (kind < 4) & ((kind & 1) == group - 2) & (j == 0)
        corner = jnp.where(kind >= 2, 2 * S, 0) + jnp.where(side == 1, S - 1, 0)
        place = jnp.where(mine, corner, place)
        valid = valid | mine
    return jnp.where(valid, place, -1)


def send_inputs_body(edges, facts, *slots):
    codes = edges[:16, SLOT:].astype(F32).astype(jnp.int32)
    row, column = lax.axis_index("core"), lax.axis_index("z") & 1
    sides = [2 - 2 * row, 2 * row, 1 + 2 * column, 3 - 2 * column]
    for g, side in enumerate(sides):
        code = jnp.where(side == 2, codes[2:3, :], codes[3:4, :])
        code = jnp.where(side == 1, codes[1:2, :], code)
        code = jnp.where(side == 0, codes[0:1, :], code)
        facts[g : g + 1, :] = jnp.full((1, SLOT), side, jnp.int32)
        facts[4 + g : 5 + g, :] = code
    hot = pick([edge_row(facts, g) for g in range(4)], 0, SLOT)
    write_slots(slots, mm(edges[:, :SLOT], hot))


def hots_body(facts, rim_one, rim_two, source_one, source_two):
    rim_one[...] = pick(rims(facts, 1), 0, FULL)
    rim_two[...] = pick(rims(facts, 2), 0, FULL)
    source_one[...] = pick(sources(facts, 1), BASE, INNER)
    source_two[...] = pick(sources(facts, 2), BASE, INNER)


def spread_body(load, spread):
    spread[...] = jnp.zeros_like(spread)
    for y in range(S):
        spread[:, BASE + PITCH * y : BASE + PITCH * y + S] = load[:, S * y : S * y + S]


def transpose_taps(src, dst, count):
    for n in range(count):
        block = src[:, C * n : C * (n + 1)].astype(F32)
        dst[:, C * n : C * (n + 1)] = jnp.transpose(block).astype(BF)


def prepare_body(load, down, one, two, upstream, grad_two, one_t, two_t, wide, col, down_t):
    transpose_taps(one, one_t, 9)
    transpose_taps(two, two_t, 9)
    transpose_taps(down, down_t, 4)
    wide[...] = jnp.zeros_like(wide)
    wide[:, BASE : BASE + INNER] = nt(load[:, S * S :], up_matrix()).astype(BF)
    for n in range(4):
        lo = BASE - (n // 2) * PITCH - n % 2
        col[C * n : C * (n + 1), :] = wide[:, lo : lo + INNER]
    upstream[...] = wide[:, BASE : BASE + INNER]
    grad_two[...] = mm(down_t[...], col[...])


def first_body(rim, source, spread, r0, r1, r2, r3, w, col, hidden, slope, m3, m2, m1, m0, wide):
    halo = nt(read_slots((r0, r1, r2, r3)), rim[...]).astype(BF)
    wide[:, BASE : BASE + FULL] = spread[...] + halo
    gather_taps(col, wide, 1, 1, BASE, INNER)
    value, grad = gelu_parts(mm(w[...], col[...]))
    value = jnp.where(columns_mask(), value, 0.0).astype(BF)
    hidden[...] = value
    slope[...] = grad
    write_slots((m3, m2, m1, m0), mm(value, source[...]))


def second_body(
    rim, hidden, r0, r1, r2, r3, w, wt, grad_two,
    ext, hidden_two, delta, grad_mid, m3, m2, m1, m0, wide, col, col_full,
):
    halo = nt(read_slots((r0, r1, r2, r3)), rim[...]).astype(BF)
    wide[:, BASE : BASE + FULL] = halo
    wide[:, 2 * BASE : 2 * BASE + INNER] = halo[:, BASE : BASE + INNER] + hidden[...]
    ext[...] = wide[:, BASE : BASE + FULL]
    gather_taps(col, wide, 2, 1, BASE, INNER)
    value, grad = gelu_parts(mm(w[...], col[...]))
    hidden_two[...] = value.astype(BF)
    back = jnp.where(columns_mask(), grad * grad_two[...], 0.0).astype(BF)
    delta[...] = back
    wide[...] = jnp.zeros_like(wide)
    wide[:, 2 * BASE : 2 * BASE + INNER] = back
    gather_taps(col_full, wide, 2, -1, 0, FULL)
    pad = mm(wt[...], col_full[...])
    grad_mid[...] = pad[:, BASE : BASE + INNER]
    write_slots((m3, m2, m1, m0), mm(pad.astype(BF), rim[...]))


def second_sums_body(scale, ext, hidden_two, delta, upstream, down, encoded, grad, grad_down, wide, col):
    wide[:, BASE : BASE + FULL] = ext[...]
    gather_taps(col, wide, 2, 1, BASE, INNER)
    grad[...] = nt(delta[...], col[...]) * scale
    wide[:, 2 * BASE : 2 * BASE + INNER] = hidden_two[...]
    for n in range(4):
        lo = 2 * BASE + (n // 2) * PITCH + n % 2
        col[C * n : C * (n + 1), :] = wide[:, lo : lo + INNER]
    four = col[: 4 * C, :]
    grad_down[...] = nt(upstream[...], four) * scale
    encoded[...] = mm(mm(down[...], four).astype(BF), up_matrix()).astype(BF)


def third_body(scale, source, grad_mid, r0, r1, r2, r3, slope, col, sum_two, sum_down, delta, packed):
    back = nt(read_slots((r0, r1, r2, r3)), source[...])
    back = (grad_mid[...] + back) * slope[...]
    back = jnp.where(columns_mask(), back, 0.0).astype(BF)
    delta[...] = back
    sums = [nt(back, col[...]) * scale, sum_two[...], sum_down[...], jnp.zeros((C, SLOT), F32)]
    sums = jnp.concatenate(sums, axis=1)
    for n in range(PACKED // C):
        packed[C * n : C * (n + 1), :] = sums[:, SLOT * n : SLOT * (n + 1)].astype(BF)


def unpack_body(packed, one, two, down):
    sums = [packed[C * n : C * (n + 1), :].astype(F32) for n in range(PACKED // C - 1)]
    sums = jnp.concatenate(sums, axis=1)
    one[...] = sums[:, : 9 * C]
    two[...] = sums[:, 9 * C : 18 * C]
    down[...] = sums[:, 18 * C :]


def fourth_body(rim, delta, wt, grad, m3, m2, m1, m0, wide, col_full):
    wide[...] = jnp.zeros_like(wide)
    wide[:, 2 * BASE : 2 * BASE + INNER] = delta[...]
    gather_taps(col_full, wide, 1, -1, 0, FULL)
    pad = mm(wt[...], col_full[...])
    grad[...] = pad[:, BASE : BASE + INNER]
    write_slots((m3, m2, m1, m0), mm(pad.astype(BF), rim[...]))


def last_body(source, grad, r0, r1, r2, r3, encoded, o):
    o[:, S * S :] = encoded[...]
    back = nt(read_slots((r0, r1, r2, r3)), source[...])
    back = (grad[...] + back).astype(BF)
    for y in range(S):
        o[:, S * y : S * y + S] = back[:, PITCH * y : PITCH * y + S]


def home(t):
    row, column = t // ROW_TILES, t % ROW_TILES
    x, y = RING[row // 2]
    return ((x * 2 + y) * 8 + column) * 2 + row % 2


def move(value, pairs):
    return lax.ppermute(value, TILE, pairs)


def swap(value, step, parity):
    count = lax.axis_size(TILE)
    pairs = []
    for t in range(count):
        if (t // step) % 2 == parity:
            here, there = home(t), home((t + step) % count)
            pairs += [(here, there), (there, here)]
    return move(value, pairs)


def lane():
    return lax.broadcasted_iota(jnp.int32, (C, SLOT), 1)


def used(message):
    return jnp.where(lane() < CORNER + 16, message, 0)


def exchange(m):
    r3 = swap(used(m[3]), 1, 1)
    r2 = swap(used(m[2]), 1, 0)
    corners = jnp.where(((lane() >> 2) & 1) == 0, r2, r3)
    r1 = swap(jnp.where(lane() < CORNER, m[1], corners), ROW_TILES, 1)
    r0 = swap(jnp.where(lane() < CORNER, m[0], corners), ROW_TILES, 0)
    return r0, r1, r2, r3


def north_south_back(m):
    r1 = swap(used(m[1]), ROW_TILES, 1)
    r0 = swap(used(m[0]), ROW_TILES, 0)
    return r0, r1, r0 + r1


def east_west_back(m, corners):
    r3 = swap(jnp.where(lane() < CORNER, m[3], corners), 1, 1)
    r2 = swap(jnp.where(lane() < CORNER, m[2], corners), 1, 0)
    return r2, r3


def exchange_back(m):
    r0, r1, corners = north_south_back(m)
    return (r0, r1) + east_west_back(m, corners)


def fold_body(parts, o):
    total = parts[0].astype(F32)
    for n in range(1, parts.shape[0]):
        total = total + parts[n].astype(F32)
    total = total.astype(BF)
    for n in range(o.shape[0]):
        o[n] = total


def trade(parts, axes):
    return lax.all_to_all(parts, axes, 0, 0, tiled=True)


def fold(parts):
    (spread,) = call(fold_body, [out(parts.shape, BF)], [], [parts], C * C, "fold")
    return spread


def per_device(inputs, cotangent, seam_codes, conv_one, conv_two, down_weight):
    x, cot = inputs[0, 0], cotangent[0, 0]
    assert lax.axis_size(TILE) == 128
    scale = 1.0 / math.sqrt(lax.axis_size(TILE + MEMBER) * S * S)

    slots = [out((C, SLOT), BF)] * 4
    wide, col = pltpu.VMEM((C, WIDE), BF), pltpu.VMEM((9 * C, INNER), BF)
    col_full = pltpu.VMEM((9 * C, FULL), BF)
    dense = 2 * C * 9 * C * INNER

    edges, load, conv_one, conv_two, down_weight = call(
        load_body,
        [out((C, 2 * SLOT), BF), out((C, LOAD), BF), out((C, 9 * C), BF), out((C, 9 * C), BF), out((C, 4 * C), BF)],
        [pltpu.SMEM((1, 4), jnp.int32), pltpu.SemaphoreType.DMA((6,))],
        [seam_codes, x, cot, conv_one, conv_two, down_weight],
        C * LOAD,
        "load",
        pltpu.HBM,
        60,
    )
    there = [(t, home(t)) for t in range(128)]
    edges, load = move(edges, there), move(load, there)
    facts, *sent = call(
        send_inputs_body, [out((8, SLOT), jnp.int32)] + slots, [], [edges], 2 * C * SLOT * 512, "send_inputs"
    )
    rim_one, rim_two, source_one, source_two = call(
        hots_body,
        [out((FULL, 512), BF)] * 2 + [out((INNER, 512), BF)] * 2,
        [],
        [facts],
        dense,
        "hots",
    )
    (spread,) = call(spread_body, [out((C, FULL), BF)], [], [load], C * FULL, "spread")
    upstream, grad_two, one_t, two_t = call(
        prepare_body,
        [out((C, INNER), BF), out((C, INNER), F32)] + [out((C, 9 * C), BF)] * 2,
        [wide, pltpu.VMEM((4 * C, INNER), BF), pltpu.VMEM((C, 4 * C), BF)],
        [load, down_weight, conv_one, conv_two],
        dense,
        "prepare",
    )
    got = exchange(sent[::-1])
    taps_one, hidden, slope, *sent = call(
        first_body,
        [out((9 * C, INNER), BF), out((C, INNER), BF), out((C, INNER), F32)] + slots,
        [wide],
        [rim_one, source_two, spread, *got, conv_one],
        2 * dense,
        "first",
    )
    got = exchange(sent[::-1])
    ext_two, hidden_two, delta_two, grad_mid, *sent = call(
        second_body,
        [out((C, FULL), BF), out((C, INNER), BF), out((C, INNER), BF), out((C, INNER), F32)] + slots,
        [wide, col, col_full],
        [rim_two, hidden, *got, conv_two, two_t, grad_two],
        3 * dense,
        "second",
    )
    got = exchange_back(sent[::-1])
    encoded, sum_two, sum_down = call(
        lambda *refs: second_sums_body(scale, *refs),
        [out((C, 256), BF), out((C, 9 * C), F32), out((C, 4 * C), F32)],
        [wide, col],
        [ext_two, hidden_two, delta_two, upstream, down_weight],
        2 * dense,
        "second_sums",
    )
    delta_one, packed = call(
        lambda *refs: third_body(scale, *refs),
        [out((C, INNER), BF), out((PACKED, SLOT), BF)],
        [],
        [source_two, grad_mid, *got, slope, taps_one, sum_two, sum_down],
        2 * dense,
        "third",
    )
    grad_in, *sent = call(
        fourth_body,
        [out((C, INNER), F32)] + slots,
        [wide, col_full],
        [rim_one, delta_one, one_t],
        2 * dense,
        "fourth",
    )
    assert lax.axis_size(NEAR) == lax.axis_size(FAR) == 16
    parts = trade(packed.reshape(16, PACKED // 16, SLOT), NEAR)
    sent = sent[::-1]
    r0, r1, corners = north_south_back(sent)
    parts = trade(fold(parts), FAR)
    r2, r3 = east_west_back(sent, corners)
    parts = trade(fold(parts), NEAR)
    (results,) = call(
        last_body, [out((C, LOAD), BF)], [], [source_one, grad_in, r0, r1, r2, r3, encoded], dense, "last"
    )
    results = move(results, [(home(t), t) for t in range(128)])
    sums = call(
        unpack_body,
        [out((C, 9 * C), F32), out((C, 9 * C), F32), out((C, 4 * C), F32)],
        [],
        [parts.reshape(PACKED, SLOT)],
        C * C,
        "unpack",
    )
    return (
        results[:, S * S :].reshape(1, 1, C, 256),
        results[:, : S * S].reshape(1, 1, C, S * S),
        *sums,
    )


def solution(mesh):
    axes = Mesh(mesh.devices.reshape(4, 2, 8, 2, 2), TILE + MEMBER)
    split = P(MEMBER, TILE, None, None)
    return jax.shard_map(
        per_device,
        mesh=axes,
        in_specs=(split, split, P(TILE, None), P(), P(), P()),
        out_specs=(split, split, P(), P(), P()),
        check_vma=False,
    )
```

```python
import math

import jax
import jax.numpy as jnp
from jax import lax
from jax.experimental import pallas as pl
from jax.experimental.pallas import tpu as pltpu
from jax.sharding import Mesh, PartitionSpec as P

S = 32
C = 64
ROW_TILES = 8
PITCH = 36
BASE = 128
INNER = S * PITCH
FULL = INNER + 2 * BASE
WIDE = FULL + 2 * BASE
SLOT = 128
PACKED = 12 * C
TILE = ("x", "y", "z", "core")
MEMBER = ("member",)
NEAR = ("z", "core")
FAR = ("x", "y", "member")
LOAD = S * S + 256
RING = ((1, 0), (0, 0), (0, 1), (1, 1), (2, 1), (3, 1), (3, 0), (2, 0))
CORNER = 64
BF = jnp.bfloat16
F32 = jnp.float32


def call(body, outs, scratch, args, flops, name, space=pltpu.VMEM, limit=24):
    specs = [pl.BlockSpec(memory_space=space) for a in args]
    moved = sum(math.prod(o.shape) * o.dtype.itemsize for o in list(outs) + list(args))
    return pl.pallas_call(
        body,
        out_shape=outs,
        in_specs=specs,
        out_specs=[pl.BlockSpec(memory_space=pltpu.VMEM)] * len(outs),
        scratch_shapes=scratch,
        compiler_params=pltpu.CompilerParams(vmem_limit_bytes=limit * 2**20),
        cost_estimate=pl.CostEstimate(flops=flops, bytes_accessed=moved, transcendentals=0),
        name=name,
    )(*args)


def out(shape, dtype):
    return jax.ShapeDtypeStruct(shape, dtype)


def nt(a, b):
    return lax.dot_general(a, b, (((1,), (1,)), ((), ())), preferred_element_type=F32)


def mm(a, b):
    return jnp.dot(a, b, preferred_element_type=F32)


def lanes_of():
    lane = lax.broadcasted_iota(jnp.int32, (1, SLOT), 1)
    part = lane - CORNER
    return lane, lane >> 5, lane & 31, part, part >> 2, part & 3


def corner_offsets(j, width):
    if width == 2:
        return j >> 1, j & 1, j >= 0
    return 0 * j, 0 * j, j == 0


def source_row(facts, group, width, pitch, base):
    lane, depth, along, part, kind, j = lanes_of()
    side, code = facts[group : group + 1, :], facts[4 + group : 5 + group, :]
    edge = (side - code + 4) & 3
    along = jnp.where((code & 1) == 1, 31 - along, along)
    near = jnp.where((edge == 1) | (edge == 2), 31 - depth, depth)
    rows = (edge & 1) == 0
    y = jnp.where(rows, near, along)
    x = jnp.where(rows, along, near)
    valid = lane < S * width
    if group >= 2:
        u, v, there = corner_offsets(j, width)
        mine = (part >= 0) & (kind < 4) & ((kind & 1) == group - 2) & there
        cy = jnp.where(kind >= 2, S - width + u, u)
        cx = jnp.where(side == 1, S - width + v, v)
        y = jnp.where(mine, cy, y)
        x = jnp.where(mine, cx, x)
        valid = valid | mine
    return jnp.where(valid, base + pitch * y + x, -1)


def rim_row(facts, group, width):
    lane, depth, along, part, kind, j = lanes_of()
    side, second = facts[group : group + 1, :], facts[2:3, :]
    beyond = jnp.where((side == 0) | (side == 3), -1 - depth, S + depth)
    rows = (side & 1) == 0
    y = jnp.where(rows, beyond, along)
    x = jnp.where(rows, along, beyond)
    valid = lane < S * width
    if group < 2:
        u, v, there = corner_offsets(j, width)
        south = jnp.where(side == 0, 1, 0)
        mine = (part >= 0) & (kind < 4) & ((kind >> 1) == south) & there
        east = jnp.where((kind & 1) == 0, second, 4 - second) == 1
        cy = jnp.where(side == 0, u - width, S + u)
        cx = jnp.where(east, S + v, v - width)
        y = jnp.where(mine, cy, y)
        x = jnp.where(mine, cx, x)
        valid = valid | mine
    return jnp.where(valid, BASE + PITCH * y + x, -1)


def pick(rows, start, count):
    row = jnp.concatenate(rows, axis=1)
    place = start + lax.broadcasted_iota(jnp.int32, (count, row.shape[1]), 0)
    return jnp.where(place == row, 1.0, 0.0).astype(BF)


def sources(facts, width, pitch=PITCH, base=BASE):
    return [source_row(facts, g, width, pitch, base) for g in range(4)]


def rims(facts, width):
    return [rim_row(facts, g, width) for g in range(4)]


def write_slots(refs, messages):
    for g, ref in zip((3, 2, 1, 0), refs, strict=True):
        ref[...] = messages[:, g * SLOT : (g + 1) * SLOT].astype(BF)


def read_slots(refs):
    return jnp.concatenate([r[...] for r in refs], axis=1)


def columns_mask():
    lane = lax.broadcasted_iota(jnp.int32, (1, INNER), 1)
    return lax.rem(lane, PITCH) < S


def taps(reach):
    return [(a - 1) * PITCH * reach + (b - 1) * reach for a in range(3) for b in range(3)]


def gelu_parts(x):
    k = math.sqrt(2.0 / math.pi)
    sq = x * x
    t = jnp.tanh(k * x * (1.0 + 0.044715 * sq))
    half = 0.5 * (1.0 + t)
    slope = half + 0.5 * x * (1.0 - t * t) * (k * (1.0 + 3.0 * 0.044715 * sq))
    return x * half, slope


def gather_taps(col, wide, reach, sign, start, count):
    for n, off in enumerate(taps(reach)):
        lo = BASE + start + sign * off
        col[C * n : C * (n + 1), :] = wide[:, lo : lo + count]


def up_matrix():
    m = lax.broadcasted_iota(jnp.int32, (1, 256), 1)
    place = lax.broadcasted_iota(jnp.int32, (INNER, 256), 0)
    return jnp.where(place == 72 * (m >> 4) + 2 * (m & 15), 1.0, 0.0).astype(BF)


def load_body(codes_hbm, x_hbm, cot_hbm, edges, load, codes, sems):
    copies = [
        pltpu.make_async_copy(codes_hbm, codes, sems.at[0]),
        pltpu.make_async_copy(x_hbm, load.at[:, pl.ds(0, S * S)], sems.at[1]),
        pltpu.make_async_copy(cot_hbm, load.at[:, pl.ds(S * S, 256)], sems.at[2]),
    ]
    for copy in copies:
        copy.start()
    lane, edge, along = lanes_of()[:3]
    y = jnp.where((edge & 1) == 0, jnp.where(edge == 0, 0, S - 1), along)
    x = jnp.where((edge & 1) == 0, along, jnp.where(edge == 1, S - 1, 0))
    hot = pick([S * y + x], 0, S * S)
    for copy in copies:
        copy.wait()
    edges[:, :SLOT] = mm(load[:, : S * S], hot).astype(BF)
    row = lax.broadcasted_iota(jnp.int32, (C, SLOT), 0)
    value = jnp.where(row == 0, codes[0, 0], jnp.where(row == 1, codes[0, 1], jnp.where(row == 2, codes[0, 2], codes[0, 3])))
    edges[:, SLOT:] = value.astype(F32).astype(BF)


def edge_row(facts, group):
    lane, _, along, part, kind, j = lanes_of()
    side, code = facts[group : group + 1, :], facts[4 + group : 5 + group, :]
    along = jnp.where((code & 1) == 1, 31 - along, along)
    place = S * ((side - code + 4) & 3) + along
    valid = lane < S
    if group >= 2:
        mine = (part >= 0) & (kind < 4) & ((kind & 1) == group - 2) & (j == 0)
        corner = jnp.where(kind >= 2, 2 * S, 0) + jnp.where(side == 1, S - 1, 0)
        place = jnp.where(mine, corner, place)
        valid = valid | mine
    return jnp.where(valid, place, -1)


def send_inputs_body(edges, facts, *slots):
    codes = edges[:16, SLOT:].astype(F32).astype(jnp.int32)
    row, column = lax.axis_index("core"), 1 - (lax.axis_index("z") & 1)
    sides = [2 - 2 * row, 2 * row, 1 + 2 * column, 3 - 2 * column]
    for g, side in enumerate(sides):
        code = jnp.where(side == 2, codes[2:3, :], codes[3:4, :])
        code = jnp.where(side == 1, codes[1:2, :], code)
        code = jnp.where(side == 0, codes[0:1, :], code)
        facts[g : g + 1, :] = jnp.full((1, SLOT), side, jnp.int32)
        facts[4 + g : 5 + g, :] = code
    hot = pick([edge_row(facts, g) for g in range(4)], 0, SLOT)
    write_slots(slots, mm(edges[:, :SLOT], hot))


def hots_body(facts, rim_one, rim_two, source_one, source_two):
    rim_one[...] = pick(rims(facts, 1), 0, FULL)
    rim_two[...] = pick(rims(facts, 2), 0, FULL)
    source_one[...] = pick(sources(facts, 1), BASE, INNER)
    source_two[...] = pick(sources(facts, 2), BASE, INNER)


def spread_body(load, one, spread, one_here):
    one_here[...] = one[...]
    spread[...] = jnp.zeros_like(spread)
    for y in range(S):
        spread[:, BASE + PITCH * y : BASE + PITCH * y + S] = load[:, S * y : S * y + S]


def transpose_taps(src, dst, count):
    for n in range(count):
        block = src[:, C * n : C * (n + 1)].astype(F32)
        dst[:, C * n : C * (n + 1)] = jnp.transpose(block).astype(BF)


def prepare_body(load, down, one, two, upstream, grad_two, one_t, two_t, wide, col, down_t):
    transpose_taps(one, one_t, 9)
    transpose_taps(two, two_t, 9)
    transpose_taps(down, down_t, 4)
    wide[...] = jnp.zeros_like(wide)
    wide[:, BASE : BASE + INNER] = nt(load[:, S * S :], up_matrix()).astype(BF)
    for n in range(4):
        lo = BASE - (n // 2) * PITCH - n % 2
        col[C * n : C * (n + 1), :] = wide[:, lo : lo + INNER]
    upstream[...] = wide[:, BASE : BASE + INNER]
    grad_two[...] = mm(down_t[...], col[...])


def first_body(rim, source, spread, r0, r1, r2, r3, w, col, hidden, slope, m3, m2, m1, m0, wide):
    halo = nt(read_slots((r0, r1, r2, r3)), rim[...]).astype(BF)
    wide[:, BASE : BASE + FULL] = spread[...] + halo
    gather_taps(col, wide, 1, 1, BASE, INNER)
    value, grad = gelu_parts(mm(w[...], col[...]))
    value = jnp.where(columns_mask(), value, 0.0).astype(BF)
    hidden[...] = value
    slope[...] = grad
    write_slots((m3, m2, m1, m0), mm(value, source[...]))


def second_body(
    rim, hidden, r0, r1, r2, r3, w, wt, grad_two,
    ext, hidden_two, delta, grad_mid, m3, m2, m1, m0, wide, col, col_full,
):
    halo = nt(read_slots((r0, r1, r2, r3)), rim[...]).astype(BF)
    wide[:, BASE : BASE + FULL] = halo
    wide[:, 2 * BASE : 2 * BASE + INNER] = halo[:, BASE : BASE + INNER] + hidden[...]
    ext[...] = wide[:, BASE : BASE + FULL]
    gather_taps(col, wide, 2, 1, BASE, INNER)
    value, grad = gelu_parts(mm(w[...], col[...]))
    hidden_two[...] = value.astype(BF)
    back = jnp.where(columns_mask(), grad * grad_two[...], 0.0).astype(BF)
    delta[...] = back
    wide[...] = jnp.zeros_like(wide)
    wide[:, 2 * BASE : 2 * BASE + INNER] = back
    gather_taps(col_full, wide, 2, -1, 0, FULL)
    pad = mm(wt[...], col_full[...])
    grad_mid[...] = pad[:, BASE : BASE + INNER]
    write_slots((m3, m2, m1, m0), mm(pad.astype(BF), rim[...]))


def second_sums_body(scale, ext, hidden_two, delta, upstream, down, encoded, grad, grad_down, wide, col):
    wide[:, BASE : BASE + FULL] = ext[...]
    gather_taps(col, wide, 2, 1, BASE, INNER)
    grad[...] = nt(delta[...], col[...]) * scale
    wide[:, 2 * BASE : 2 * BASE + INNER] = hidden_two[...]
    for n in range(4):
        lo = 2 * BASE + (n // 2) * PITCH + n % 2
        col[C * n : C * (n + 1), :] = wide[:, lo : lo + INNER]
    four = col[: 4 * C, :]
    grad_down[...] = nt(upstream[...], four) * scale
    encoded[...] = mm(mm(down[...], four).astype(BF), up_matrix()).astype(BF)


def third_body(scale, source, grad_mid, r0, r1, r2, r3, slope, col, sum_two, sum_down, delta, packed):
    back = nt(read_slots((r0, r1, r2, r3)), source[...])
    back = (grad_mid[...] + back) * slope[...]
    back = jnp.where(columns_mask(), back, 0.0).astype(BF)
    delta[...] = back
    sums = [nt(back, col[...]) * scale, sum_two[...], sum_down[...], jnp.zeros((C, SLOT), F32)]
    sums = jnp.concatenate(sums, axis=1)
    for n in range(PACKED // C):
        packed[C * n : C * (n + 1), :] = sums[:, SLOT * n : SLOT * (n + 1)].astype(BF)


def unpack_body(packed, one, two, down):
    sums = [packed[C * n : C * (n + 1), :].astype(F32) for n in range(PACKED // C - 1)]
    sums = jnp.concatenate(sums, axis=1)
    one[...] = sums[:, : 9 * C]
    two[...] = sums[:, 9 * C : 18 * C]
    down[...] = sums[:, 18 * C :]


def fourth_body(rim, delta, wt, grad, m3, m2, m1, m0, wide, col_full):
    wide[...] = jnp.zeros_like(wide)
    wide[:, 2 * BASE : 2 * BASE + INNER] = delta[...]
    gather_taps(col_full, wide, 1, -1, 0, FULL)
    pad = mm(wt[...], col_full[...])
    grad[...] = pad[:, BASE : BASE + INNER]
    write_slots((m3, m2, m1, m0), mm(pad.astype(BF), rim[...]))


def last_body(source, grad, r0, r1, r2, r3, encoded, o):
    o[:, S * S :] = encoded[...]
    back = nt(read_slots((r0, r1, r2, r3)), source[...])
    back = (grad[...] + back).astype(BF)
    for y in range(S):
        o[:, S * y : S * y + S] = back[:, PITCH * y : PITCH * y + S]


def home(t):
    row, column = t // ROW_TILES, t % ROW_TILES
    x, y = RING[row // 2]
    return ((x * 2 + y) * 8 + 7 - column) * 2 + row % 2


def move(value, pairs):
    return lax.ppermute(value, TILE, pairs)


def swap(value, step, parity):
    count = lax.axis_size(TILE)
    pairs = []
    for t in range(count):
        if (t // step) % 2 == parity:
            here, there = home(t), home((t + step) % count)
            pairs += [(here, there), (there, here)]
    return move(value, pairs)


def lane():
    return lax.broadcasted_iota(jnp.int32, (C, SLOT), 1)


def used(message):
    return jnp.where(lane() < CORNER + 16, message, 0)


def exchange(m, done=()):
    r3 = swap(used(m[3]), 1, 1)
    r2 = swap(used(m[2]), 1, 0)
    corners = jnp.where(((lane() >> 2) & 1) == 0, r2, r3)
    if done:
        corners, done = lax.optimization_barrier((corners, done))
    r1 = swap(jnp.where(lane() < CORNER, m[1], corners), ROW_TILES, 1)
    r0 = swap(jnp.where(lane() < CORNER, m[0], corners), ROW_TILES, 0)
    return (r0, r1, r2, r3), done


def north_south_back(m):
    r1 = swap(used(m[1]), ROW_TILES, 1)
    r0 = swap(used(m[0]), ROW_TILES, 0)
    return r0, r1, r0 + r1


def east_west_back(m, corners):
    r3 = swap(jnp.where(lane() < CORNER, m[3], corners), 1, 1)
    r2 = swap(jnp.where(lane() < CORNER, m[2], corners), 1, 0)
    return r2, r3


def exchange_back(m):
    r0, r1, corners = north_south_back(m)
    return (r0, r1) + east_west_back(m, corners)


def fold_body(parts, o):
    total = parts[0].astype(F32)
    for n in range(1, parts.shape[0]):
        total = total + parts[n].astype(F32)
    total = total.astype(BF)
    for n in range(o.shape[0]):
        o[n] = total


def trade(parts, axes):
    return lax.all_to_all(parts, axes, 0, 0, tiled=True)


def fold(parts):
    (spread,) = call(fold_body, [out(parts.shape, BF)], [], [parts], C * C, "fold")
    return spread


def per_device(inputs, cotangent, seam_codes, conv_one, conv_two, down_weight):
    x, cot = inputs[0, 0], cotangent[0, 0]
    assert lax.axis_size(TILE) == 128
    scale = 1.0 / math.sqrt(lax.axis_size(TILE + MEMBER) * S * S)

    slots = [out((C, SLOT), BF)] * 4
    wide, col = pltpu.VMEM((C, WIDE), BF), pltpu.VMEM((9 * C, INNER), BF)
    col_full = pltpu.VMEM((9 * C, FULL), BF)
    dense = 2 * C * 9 * C * INNER

    edges, load = call(
        load_body,
        [out((C, 2 * SLOT), BF), out((C, LOAD), BF)],
        [pltpu.SMEM((1, 4), jnp.int32), pltpu.SemaphoreType.DMA((3,))],
        [seam_codes, x, cot],
        C * LOAD,
        "load",
        pltpu.HBM,
        60,
    )
    there = [(t, home(t)) for t in range(128)]
    edges, load = move(edges, there), move(load, there)
    facts, *sent = call(
        send_inputs_body, [out((8, SLOT), jnp.int32)] + slots, [], [edges], 2 * C * SLOT * 512, "send_inputs"
    )
    hots = call(
        hots_body,
        [out((FULL, 512), BF)] * 2 + [out((INNER, 512), BF)] * 2,
        [],
        [facts],
        dense,
        "hots",
    )
    got, hots = exchange(sent[::-1], hots)
    rim_one, rim_two, source_one, source_two = hots
    spread, conv_one = call(
        spread_body, [out((C, FULL), BF), out((C, 9 * C), BF)], [], [load, conv_one], C * FULL, "spread"
    )
    upstream, grad_two, one_t, two_t = call(
        prepare_body,
        [out((C, INNER), BF), out((C, INNER), F32)] + [out((C, 9 * C), BF)] * 2,
        [wide, pltpu.VMEM((4 * C, INNER), BF), pltpu.VMEM((C, 4 * C), BF)],
        [load, down_weight, conv_one, conv_two],
        dense,
        "prepare",
    )
    taps_one, hidden, slope, *sent = call(
        first_body,
        [out((9 * C, INNER), BF), out((C, INNER), BF), out((C, INNER), F32)] + slots,
        [wide],
        [rim_one, source_two, spread, *got, conv_one],
        2 * dense,
        "first",
    )
    got, _ = exchange(sent[::-1])
    ext_two, hidden_two, delta_two, grad_mid, *sent = call(
        second_body,
        [out((C, FULL), BF), out((C, INNER), BF), out((C, INNER), BF), out((C, INNER), F32)] + slots,
        [wide, col, col_full],
        [rim_two, hidden, *got, conv_two, two_t, grad_two],
        3 * dense,
        "second",
    )
    got = exchange_back(sent[::-1])
    encoded, sum_two, sum_down = call(
        lambda *refs: second_sums_body(scale, *refs),
        [out((C, 256), BF), out((C, 9 * C), F32), out((C, 4 * C), F32)],
        [wide, col],
        [ext_two, hidden_two, delta_two, upstream, down_weight],
        2 * dense,
        "second_sums",
    )
    delta_one, packed = call(
        lambda *refs: third_body(scale, *refs),
        [out((C, INNER), BF), out((PACKED, SLOT), BF)],
        [],
        [source_two, grad_mid, *got, slope, taps_one, sum_two, sum_down],
        2 * dense,
        "third",
    )
    grad_in, *sent = call(
        fourth_body,
        [out((C, INNER), F32)] + slots,
        [wide, col_full],
        [rim_one, delta_one, one_t],
        2 * dense,
        "fourth",
    )
    assert lax.axis_size(NEAR) == lax.axis_size(FAR) == 16
    parts = trade(packed.reshape(16, PACKED // 16, SLOT), NEAR)
    sent = sent[::-1]
    r0, r1, corners = north_south_back(sent)
    parts = trade(fold(parts), FAR)
    r2, r3 = east_west_back(sent, corners)
    parts = trade(fold(parts), NEAR)
    (results,) = call(
        last_body, [out((C, LOAD), BF)], [], [source_one, grad_in, r0, r1, r2, r3, encoded], dense, "last"
    )
    results = move(results, [(home(t), t) for t in range(128)])
    sums = call(
        unpack_body,
        [out((C, 9 * C), F32), out((C, 9 * C), F32), out((C, 4 * C), F32)],
        [],
        [parts.reshape(PACKED, SLOT)],
        C * C,
        "unpack",
    )
    return (
        results[:, S * S :].reshape(1, 1, C, 256),
        results[:, : S * S].reshape(1, 1, C, S * S),
        *sums,
    )


def solution(mesh):
    axes = Mesh(mesh.devices.reshape(4, 2, 8, 2, 2), TILE + MEMBER)
    split = P(MEMBER, TILE, None, None)
    return jax.shard_map(
        per_device,
        mesh=axes,
        in_specs=(split, split, P(TILE, None), P(), P(), P()),
        out_specs=(split, split, P(), P(), P()),
        check_vma=False,
    )
```

```python
import math

import jax
import jax.numpy as jnp
from jax import lax
from jax.experimental import pallas as pl
from jax.experimental.pallas import tpu as pltpu
from jax.sharding import Mesh, PartitionSpec as P

S = 32
C = 64
ROW_TILES = 8
PITCH = 36
BASE = 128
INNER = S * PITCH
FULL = INNER + 2 * BASE
WIDE = FULL + 2 * BASE
SLOT = 128
PACKED = 12 * C
TILE = ("x", "y", "z", "core")
MEMBER = ("member",)
NEAR = ("core", "z")
FAR = ("member", "x", "y")
LOAD = S * S + 256
RING = ((1, 0), (0, 0), (0, 1), (1, 1), (2, 1), (3, 1), (3, 0), (2, 0))
CORNER = 64
BF = jnp.bfloat16
F32 = jnp.float32


def call(body, outs, scratch, args, flops, name, space=pltpu.VMEM, limit=24):
    specs = [pl.BlockSpec(memory_space=space) for a in args]
    moved = sum(math.prod(o.shape) * o.dtype.itemsize for o in list(outs) + list(args))
    return pl.pallas_call(
        body,
        out_shape=outs,
        in_specs=specs,
        out_specs=[pl.BlockSpec(memory_space=pltpu.VMEM)] * len(outs),
        scratch_shapes=scratch,
        compiler_params=pltpu.CompilerParams(vmem_limit_bytes=limit * 2**20),
        cost_estimate=pl.CostEstimate(flops=flops, bytes_accessed=moved, transcendentals=0),
        name=name,
    )(*args)


def out(shape, dtype):
    return jax.ShapeDtypeStruct(shape, dtype)


def nt(a, b):
    return lax.dot_general(a, b, (((1,), (1,)), ((), ())), preferred_element_type=F32)


def mm(a, b):
    return jnp.dot(a, b, preferred_element_type=F32)


def lanes_of():
    lane = lax.broadcasted_iota(jnp.int32, (1, SLOT), 1)
    part = lane - CORNER
    return lane, lane >> 5, lane & 31, part, part >> 2, part & 3


def corner_offsets(j, width):
    if width == 2:
        return j >> 1, j & 1, j >= 0
    return 0 * j, 0 * j, j == 0


def source_row(facts, group, width, pitch, base):
    lane, depth, along, part, kind, j = lanes_of()
    side, code = facts[group : group + 1, :], facts[4 + group : 5 + group, :]
    edge = (side - code + 4) & 3
    along = jnp.where((code & 1) == 1, 31 - along, along)
    near = jnp.where((edge == 1) | (edge == 2), 31 - depth, depth)
    rows = (edge & 1) == 0
    y = jnp.where(rows, near, along)
    x = jnp.where(rows, along, near)
    valid = lane < S * width
    if group >= 2:
        u, v, there = corner_offsets(j, width)
        mine = (part >= 0) & (kind < 4) & ((kind & 1) == group - 2) & there
        cy = jnp.where(kind >= 2, S - width + u, u)
        cx = jnp.where(side == 1, S - width + v, v)
        y = jnp.where(mine, cy, y)
        x = jnp.where(mine, cx, x)
        valid = valid | mine
    return jnp.where(valid, base + pitch * y + x, -1)


def rim_row(facts, group, width):
    lane, depth, along, part, kind, j = lanes_of()
    side, second = facts[group : group + 1, :], facts[2:3, :]
    beyond = jnp.where((side == 0) | (side == 3), -1 - depth, S + depth)
    rows = (side & 1) == 0
    y = jnp.where(rows, beyond, along)
    x = jnp.where(rows, along, beyond)
    valid = lane < S * width
    if group < 2:
        u, v, there = corner_offsets(j, width)
        south = jnp.where(side == 0, 1, 0)
        mine = (part >= 0) & (kind < 4) & ((kind >> 1) == south) & there
        east = jnp.where((kind & 1) == 0, second, 4 - second) == 1
        cy = jnp.where(side == 0, u - width, S + u)
        cx = jnp.where(east, S + v, v - width)
        y = jnp.where(mine, cy, y)
        x = jnp.where(mine, cx, x)
        valid = valid | mine
    return jnp.where(valid, BASE + PITCH * y + x, -1)


def pick(rows, start, count):
    row = jnp.concatenate(rows, axis=1)
    place = start + lax.broadcasted_iota(jnp.int32, (count, row.shape[1]), 0)
    return jnp.where(place == row, 1.0, 0.0).astype(BF)


def sources(facts, width, pitch=PITCH, base=BASE):
    return [source_row(facts, g, width, pitch, base) for g in range(4)]


def rims(facts, width):
    return [rim_row(facts, g, width) for g in range(4)]


def write_slots(refs, messages):
    for g, ref in zip((3, 2, 1, 0), refs, strict=True):
        ref[...] = messages[:, g * SLOT : (g + 1) * SLOT].astype(BF)


def read_slots(refs):
    return jnp.concatenate([r[...] for r in refs], axis=1)


def columns_mask():
    lane = lax.broadcasted_iota(jnp.int32, (1, INNER), 1)
    return lax.rem(lane, PITCH) < S


def taps(reach):
    return [(a - 1) * PITCH * reach + (b - 1) * reach for a in range(3) for b in range(3)]


def gelu_parts(x):
    k = math.sqrt(2.0 / math.pi)
    sq = x * x
    t = jnp.tanh(k * x * (1.0 + 0.044715 * sq))
    half = 0.5 * (1.0 + t)
    slope = half + 0.5 * x * (1.0 - t * t) * (k * (1.0 + 3.0 * 0.044715 * sq))
    return x * half, slope


def gather_taps(col, wide, reach, sign, start, count):
    for n, off in enumerate(taps(reach)):
        lo = BASE + start + sign * off
        col[C * n : C * (n + 1), :] = wide[:, lo : lo + count]


def up_matrix():
    m = lax.broadcasted_iota(jnp.int32, (1, 256), 1)
    place = lax.broadcasted_iota(jnp.int32, (INNER, 256), 0)
    return jnp.where(place == 72 * (m >> 4) + 2 * (m & 15), 1.0, 0.0).astype(BF)


def load_body(codes_hbm, x_hbm, cot_hbm, edges, load, codes, sems):
    copies = [
        pltpu.make_async_copy(codes_hbm, codes, sems.at[0]),
        pltpu.make_async_copy(x_hbm, load.at[:, pl.ds(0, S * S)], sems.at[1]),
        pltpu.make_async_copy(cot_hbm, load.at[:, pl.ds(S * S, 256)], sems.at[2]),
    ]
    for copy in copies:
        copy.start()
    lane, edge, along = lanes_of()[:3]
    y = jnp.where((edge & 1) == 0, jnp.where(edge == 0, 0, S - 1), along)
    x = jnp.where((edge & 1) == 0, along, jnp.where(edge == 1, S - 1, 0))
    hot = pick([S * y + x], 0, S * S)
    for copy in copies:
        copy.wait()
    edges[:, :SLOT] = mm(load[:, : S * S], hot).astype(BF)
    row = lax.broadcasted_iota(jnp.int32, (C, SLOT), 0)
    value = jnp.where(row == 0, codes[0, 0], jnp.where(row == 1, codes[0, 1], jnp.where(row == 2, codes[0, 2], codes[0, 3])))
    edges[:, SLOT:] = value.astype(F32).astype(BF)


def edge_row(facts, group):
    lane, _, along, part, kind, j = lanes_of()
    side, code = facts[group : group + 1, :], facts[4 + group : 5 + group, :]
    along = jnp.where((code & 1) == 1, 31 - along, along)
    place = S * ((side - code + 4) & 3) + along
    valid = lane < S
    if group >= 2:
        mine = (part >= 0) & (kind < 4) & ((kind & 1) == group - 2) & (j == 0)
        corner = jnp.where(kind >= 2, 2 * S, 0) + jnp.where(side == 1, S - 1, 0)
        place = jnp.where(mine, corner, place)
        valid = valid | mine
    return jnp.where(valid, place, -1)


def send_inputs_body(edges, facts, *slots):
    codes = edges[:16, SLOT:].astype(F32).astype(jnp.int32)
    row, column = lax.axis_index("core"), 1 - (lax.axis_index("z") & 1)
    sides = [2 - 2 * row, 2 * row, 1 + 2 * column, 3 - 2 * column]
    for g, side in enumerate(sides):
        code = jnp.where(side == 2, codes[2:3, :], codes[3:4, :])
        code = jnp.where(side == 1, codes[1:2, :], code)
        code = jnp.where(side == 0, codes[0:1, :], code)
        facts[g : g + 1, :] = jnp.full((1, SLOT), side, jnp.int32)
        facts[4 + g : 5 + g, :] = code
    hot = pick([edge_row(facts, g) for g in range(4)], 0, SLOT)
    write_slots(slots, mm(edges[:, :SLOT], hot))


def hots_body(facts, rim_one, rim_two, source_one, source_two):
    rim_one[...] = pick(rims(facts, 1), 0, FULL)
    rim_two[...] = pick(rims(facts, 2), 0, FULL)
    source_one[...] = pick(sources(facts, 1), BASE, INNER)
    source_two[...] = pick(sources(facts, 2), BASE, INNER)


def spread_body(load, one, spread, one_here):
    one_here[...] = one[...]
    spread[...] = jnp.zeros_like(spread)
    for y in range(S):
        spread[:, BASE + PITCH * y : BASE + PITCH * y + S] = load[:, S * y : S * y + S]


def transpose_taps(src, dst, count):
    for n in range(count):
        block = src[:, C * n : C * (n + 1)].astype(F32)
        dst[:, C * n : C * (n + 1)] = jnp.transpose(block).astype(BF)


def prepare_body(load, down, one, two, upstream, grad_two, one_t, two_t, wide, col, down_t):
    transpose_taps(one, one_t, 9)
    transpose_taps(two, two_t, 9)
    transpose_taps(down, down_t, 4)
    wide[...] = jnp.zeros_like(wide)
    wide[:, BASE : BASE + INNER] = nt(load[:, S * S :], up_matrix()).astype(BF)
    for n in range(4):
        lo = BASE - (n // 2) * PITCH - n % 2
        col[C * n : C * (n + 1), :] = wide[:, lo : lo + INNER]
    upstream[...] = wide[:, BASE : BASE + INNER]
    grad_two[...] = mm(down_t[...], col[...])


def first_body(rim, source, spread, r0, r1, r2, r3, w, col, hidden, slope, m3, m2, m1, m0, wide):
    halo = nt(read_slots((r0, r1, r2, r3)), rim[...]).astype(BF)
    wide[:, BASE : BASE + FULL] = spread[...] + halo
    gather_taps(col, wide, 1, 1, BASE, INNER)
    value, grad = gelu_parts(mm(w[...], col[...]))
    value = jnp.where(columns_mask(), value, 0.0).astype(BF)
    hidden[...] = value
    slope[...] = grad
    write_slots((m3, m2, m1, m0), mm(value, source[...]))


def second_body(
    rim, hidden, r0, r1, r2, r3, w, wt, grad_two,
    ext, hidden_two, delta, grad_mid, m3, m2, m1, m0, wide, col, col_full,
):
    halo = nt(read_slots((r0, r1, r2, r3)), rim[...]).astype(BF)
    wide[:, BASE : BASE + FULL] = halo
    wide[:, 2 * BASE : 2 * BASE + INNER] = halo[:, BASE : BASE + INNER] + hidden[...]
    ext[...] = wide[:, BASE : BASE + FULL]
    gather_taps(col, wide, 2, 1, BASE, INNER)
    value, grad = gelu_parts(mm(w[...], col[...]))
    hidden_two[...] = value.astype(BF)
    back = jnp.where(columns_mask(), grad * grad_two[...], 0.0).astype(BF)
    delta[...] = back
    wide[...] = jnp.zeros_like(wide)
    wide[:, 2 * BASE : 2 * BASE + INNER] = back
    gather_taps(col_full, wide, 2, -1, 0, FULL)
    pad = mm(wt[...], col_full[...])
    grad_mid[...] = pad[:, BASE : BASE + INNER]
    write_slots((m3, m2, m1, m0), mm(pad.astype(BF), rim[...]))


def second_sums_body(scale, ext, hidden_two, delta, upstream, down, encoded, grad, grad_down, wide, col):
    wide[:, BASE : BASE + FULL] = ext[...]
    gather_taps(col, wide, 2, 1, BASE, INNER)
    grad[...] = nt(delta[...], col[...]) * scale
    wide[:, 2 * BASE : 2 * BASE + INNER] = hidden_two[...]
    for n in range(4):
        lo = 2 * BASE + (n // 2) * PITCH + n % 2
        col[C * n : C * (n + 1), :] = wide[:, lo : lo + INNER]
    four = col[: 4 * C, :]
    grad_down[...] = nt(upstream[...], four) * scale
    encoded[...] = mm(mm(down[...], four).astype(BF), up_matrix()).astype(BF)


def third_body(scale, source, grad_mid, r0, r1, r2, r3, slope, col, sum_two, sum_down, delta, packed):
    back = nt(read_slots((r0, r1, r2, r3)), source[...])
    back = (grad_mid[...] + back) * slope[...]
    back = jnp.where(columns_mask(), back, 0.0).astype(BF)
    delta[...] = back
    sums = [nt(back, col[...]) * scale, sum_two[...], sum_down[...], jnp.zeros((C, SLOT), F32)]
    sums = jnp.concatenate(sums, axis=1)
    for n in range(PACKED // C):
        packed[C * n : C * (n + 1), :] = sums[:, SLOT * n : SLOT * (n + 1)].astype(BF)


def unpack_body(packed, one, two, down):
    sums = [packed[C * n : C * (n + 1), :].astype(F32) for n in range(PACKED // C - 1)]
    sums = jnp.concatenate(sums, axis=1)
    one[...] = sums[:, : 9 * C]
    two[...] = sums[:, 9 * C : 18 * C]
    down[...] = sums[:, 18 * C :]


def fourth_body(rim, delta, wt, grad, m3, m2, m1, m0, wide, col_full):
    wide[...] = jnp.zeros_like(wide)
    wide[:, 2 * BASE : 2 * BASE + INNER] = delta[...]
    gather_taps(col_full, wide, 1, -1, 0, FULL)
    pad = mm(wt[...], col_full[...])
    grad[...] = pad[:, BASE : BASE + INNER]
    write_slots((m3, m2, m1, m0), mm(pad.astype(BF), rim[...]))


def last_body(source, grad, r0, r1, r2, r3, encoded, o):
    o[:, S * S :] = encoded[...]
    back = nt(read_slots((r0, r1, r2, r3)), source[...])
    back = (grad[...] + back).astype(BF)
    for y in range(S):
        o[:, S * y : S * y + S] = back[:, PITCH * y : PITCH * y + S]


def home(t):
    row, column = t // ROW_TILES, t % ROW_TILES
    x, y = RING[row // 2]
    return ((x * 2 + y) * 8 + 7 - column) * 2 + row % 2


def move(value, pairs):
    return lax.ppermute(value, TILE, pairs)


def swap(value, step, parity):
    count = lax.axis_size(TILE)
    pairs = []
    for t in range(count):
        if (t // step) % 2 == parity:
            here, there = home(t), home((t + step) % count)
            pairs += [(here, there), (there, here)]
    return move(value, pairs)


def lane():
    return lax.broadcasted_iota(jnp.int32, (C, SLOT), 1)


def used(message):
    return jnp.where(lane() < CORNER + 16, message, 0)


def exchange(m, done=()):
    r3 = swap(used(m[3]), 1, 1)
    r2 = swap(used(m[2]), 1, 0)
    corners = jnp.where(((lane() >> 2) & 1) == 0, r2, r3)
    if done:
        corners, done = lax.optimization_barrier((corners, done))
    r1 = swap(jnp.where(lane() < CORNER, m[1], corners), ROW_TILES, 1)
    r0 = swap(jnp.where(lane() < CORNER, m[0], corners), ROW_TILES, 0)
    return (r0, r1, r2, r3), done


def north_south_back(m):
    r1 = swap(used(m[1]), ROW_TILES, 1)
    r0 = swap(used(m[0]), ROW_TILES, 0)
    return r0, r1, r0 + r1


def east_west_back(m, corners):
    r3 = swap(jnp.where(lane() < CORNER, m[3], corners), 1, 1)
    r2 = swap(jnp.where(lane() < CORNER, m[2], corners), 1, 0)
    return r2, r3


def exchange_back(m):
    r0, r1, corners = north_south_back(m)
    return (r0, r1) + east_west_back(m, corners)


def fold_body(parts, o):
    total = parts[0].astype(F32)
    for n in range(1, parts.shape[0]):
        total = total + parts[n].astype(F32)
    total = total.astype(BF)
    for n in range(o.shape[0]):
        o[n] = total


def trade(parts, axes):
    return lax.all_to_all(parts, axes, 0, 0, tiled=True)


def fold(parts):
    (spread,) = call(fold_body, [out(parts.shape, BF)], [], [parts], C * C, "fold")
    return spread


def per_device(inputs, cotangent, seam_codes, conv_one, conv_two, down_weight):
    x, cot = inputs[0, 0], cotangent[0, 0]
    assert lax.axis_size(TILE) == 128
    scale = 1.0 / math.sqrt(lax.axis_size(TILE + MEMBER) * S * S)

    slots = [out((C, SLOT), BF)] * 4
    wide, col = pltpu.VMEM((C, WIDE), BF), pltpu.VMEM((9 * C, INNER), BF)
    col_full = pltpu.VMEM((9 * C, FULL), BF)
    dense = 2 * C * 9 * C * INNER

    edges, load = call(
        load_body,
        [out((C, 2 * SLOT), BF), out((C, LOAD), BF)],
        [pltpu.SMEM((1, 4), jnp.int32), pltpu.SemaphoreType.DMA((3,))],
        [seam_codes, x, cot],
        C * LOAD,
        "load",
        pltpu.HBM,
        60,
    )
    there = [(t, home(t)) for t in range(128)]
    edges, load = move(edges, there), move(load, there)
    facts, *sent = call(
        send_inputs_body, [out((8, SLOT), jnp.int32)] + slots, [], [edges], 2 * C * SLOT * 512, "send_inputs"
    )
    hots = call(
        hots_body,
        [out((FULL, 512), BF)] * 2 + [out((INNER, 512), BF)] * 2,
        [],
        [facts],
        dense,
        "hots",
    )
    got, hots = exchange(sent[::-1], hots)
    rim_one, rim_two, source_one, source_two = hots
    spread, conv_one = call(
        spread_body, [out((C, FULL), BF), out((C, 9 * C), BF)], [], [load, conv_one], C * FULL, "spread"
    )
    upstream, grad_two, one_t, two_t = call(
        prepare_body,
        [out((C, INNER), BF), out((C, INNER), F32)] + [out((C, 9 * C), BF)] * 2,
        [wide, pltpu.VMEM((4 * C, INNER), BF), pltpu.VMEM((C, 4 * C), BF)],
        [load, down_weight, conv_one, conv_two],
        dense,
        "prepare",
    )
    taps_one, hidden, slope, *sent = call(
        first_body,
        [out((9 * C, INNER), BF), out((C, INNER), BF), out((C, INNER), F32)] + slots,
        [wide],
        [rim_one, source_two, spread, *got, conv_one],
        2 * dense,
        "first",
    )
    got, _ = exchange(sent[::-1])
    ext_two, hidden_two, delta_two, grad_mid, *sent = call(
        second_body,
        [out((C, FULL), BF), out((C, INNER), BF), out((C, INNER), BF), out((C, INNER), F32)] + slots,
        [wide, col, col_full],
        [rim_two, hidden, *got, conv_two, two_t, grad_two],
        3 * dense,
        "second",
    )
    got = exchange_back(sent[::-1])
    encoded, sum_two, sum_down = call(
        lambda *refs: second_sums_body(scale, *refs),
        [out((C, 256), BF), out((C, 9 * C), F32), out((C, 4 * C), F32)],
        [wide, col],
        [ext_two, hidden_two, delta_two, upstream, down_weight],
        2 * dense,
        "second_sums",
    )
    delta_one, packed = call(
        lambda *refs: third_body(scale, *refs),
        [out((C, INNER), BF), out((PACKED, SLOT), BF)],
        [],
        [source_two, grad_mid, *got, slope, taps_one, sum_two, sum_down],
        2 * dense,
        "third",
    )
    grad_in, *sent = call(
        fourth_body,
        [out((C, INNER), F32)] + slots,
        [wide, col_full],
        [rim_one, delta_one, one_t],
        2 * dense,
        "fourth",
    )
    assert lax.axis_size(NEAR) == lax.axis_size(FAR) == 16
    parts = trade(packed.reshape(16, PACKED // 16, SLOT), NEAR)
    sent = sent[::-1]
    r0, r1, corners = north_south_back(sent)
    parts = trade(fold(parts), FAR)
    r2, r3 = east_west_back(sent, corners)
    parts = trade(fold(parts), NEAR)
    (results,) = call(
        last_body, [out((C, LOAD), BF)], [], [source_one, grad_in, r0, r1, r2, r3, encoded], dense, "last"
    )
    results = move(results, [(home(t), t) for t in range(128)])
    sums = call(
        unpack_body,
        [out((C, 9 * C), F32), out((C, 9 * C), F32), out((C, 4 * C), F32)],
        [],
        [parts.reshape(PACKED, SLOT)],
        C * C,
        "unpack",
    )
    return (
        results[:, S * S :].reshape(1, 1, C, 256),
        results[:, : S * S].reshape(1, 1, C, S * S),
        *sums,
    )


def solution(mesh):
    axes = Mesh(mesh.devices.reshape(4, 2, 8, 2, 2), TILE + MEMBER)
    split = P(MEMBER, TILE, None, None)
    return jax.shard_map(
        per_device,
        mesh=axes,
        in_specs=(split, split, P(TILE, None), P(), P(), P()),
        out_specs=(split, split, P(), P(), P()),
        check_vma=False,
    )
```

```python
import math

import jax
import jax.numpy as jnp
from jax import lax
from jax.experimental import pallas as pl
from jax.experimental.pallas import tpu as pltpu
from jax.sharding import Mesh, PartitionSpec as P

S = 32
C = 64
ROW_TILES = 8
PITCH = 36
BASE = 128
INNER = S * PITCH
FULL = INNER + 2 * BASE
WIDE = FULL + 2 * BASE
SLOT = 128
PACKED = 12 * C
TILE = ("x", "y", "z", "core")
MEMBER = ("member",)
NEAR = ("core", "z")
FAR = ("member", "x", "y")
LOAD = S * S + 256
RING = ((1, 0), (0, 0), (0, 1), (1, 1), (2, 1), (3, 1), (3, 0), (2, 0))
CORNER = 64
BF = jnp.bfloat16
F32 = jnp.float32


def call(body, outs, scratch, args, flops, name, space=pltpu.VMEM, limit=24, last=pltpu.VMEM):
    specs = [pl.BlockSpec(memory_space=space) for a in args]
    moved = sum(math.prod(o.shape) * o.dtype.itemsize for o in list(outs) + list(args))
    return pl.pallas_call(
        body,
        out_shape=outs,
        in_specs=specs,
        out_specs=[pl.BlockSpec(memory_space=pltpu.VMEM)] * (len(outs) - 1) + [pl.BlockSpec(memory_space=last)],
        scratch_shapes=scratch,
        compiler_params=pltpu.CompilerParams(vmem_limit_bytes=limit * 2**20),
        cost_estimate=pl.CostEstimate(flops=flops, bytes_accessed=moved, transcendentals=0),
        name=name,
    )(*args)


def out(shape, dtype):
    return jax.ShapeDtypeStruct(shape, dtype)


def nt(a, b):
    return lax.dot_general(a, b, (((1,), (1,)), ((), ())), preferred_element_type=F32)


def mm(a, b):
    return jnp.dot(a, b, preferred_element_type=F32)


def lanes_of():
    lane = lax.broadcasted_iota(jnp.int32, (1, SLOT), 1)
    part = lane - CORNER
    return lane, lane >> 5, lane & 31, part, part >> 2, part & 3


def corner_offsets(j, width):
    if width == 2:
        return j >> 1, j & 1, j >= 0
    return 0 * j, 0 * j, j == 0


def source_row(facts, group, width, pitch, base):
    lane, depth, along, part, kind, j = lanes_of()
    side, code = facts[group : group + 1, :], facts[4 + group : 5 + group, :]
    edge = (side - code + 4) & 3
    along = jnp.where((code & 1) == 1, 31 - along, along)
    near = jnp.where((edge == 1) | (edge == 2), 31 - depth, depth)
    rows = (edge & 1) == 0
    y = jnp.where(rows, near, along)
    x = jnp.where(rows, along, near)
    valid = lane < S * width
    if group >= 2:
        u, v, there = corner_offsets(j, width)
        mine = (part >= 0) & (kind < 4) & ((kind & 1) == group - 2) & there
        cy = jnp.where(kind >= 2, S - width + u, u)
        cx = jnp.where(side == 1, S - width + v, v)
        y = jnp.where(mine, cy, y)
        x = jnp.where(mine, cx, x)
        valid = valid | mine
    return jnp.where(valid, base + pitch * y + x, -1)


def rim_row(facts, group, width):
    lane, depth, along, part, kind, j = lanes_of()
    side, second = facts[group : group + 1, :], facts[2:3, :]
    beyond = jnp.where((side == 0) | (side == 3), -1 - depth, S + depth)
    rows = (side & 1) == 0
    y = jnp.where(rows, beyond, along)
    x = jnp.where(rows, along, beyond)
    valid = lane < S * width
    if group < 2:
        u, v, there = corner_offsets(j, width)
        south = jnp.where(side == 0, 1, 0)
        mine = (part >= 0) & (kind < 4) & ((kind >> 1) == south) & there
        east = jnp.where((kind & 1) == 0, second, 4 - second) == 1
        cy = jnp.where(side == 0, u - width, S + u)
        cx = jnp.where(east, S + v, v - width)
        y = jnp.where(mine, cy, y)
        x = jnp.where(mine, cx, x)
        valid = valid | mine
    return jnp.where(valid, BASE + PITCH * y + x, -1)


def pick(rows, start, count):
    row = jnp.concatenate(rows, axis=1)
    place = start + lax.broadcasted_iota(jnp.int32, (count, row.shape[1]), 0)
    return jnp.where(place == row, 1.0, 0.0).astype(BF)


def sources(facts, width, pitch=PITCH, base=BASE):
    return [source_row(facts, g, width, pitch, base) for g in range(4)]


def rims(facts, width):
    return [rim_row(facts, g, width) for g in range(4)]


def write_slots(refs, messages):
    for g, ref in zip((3, 2, 1, 0), refs, strict=True):
        ref[...] = messages[:, g * SLOT : (g + 1) * SLOT].astype(BF)


def read_slots(refs):
    return jnp.concatenate([r[...] for r in refs], axis=1)


def columns_mask():
    lane = lax.broadcasted_iota(jnp.int32, (1, INNER), 1)
    return lax.rem(lane, PITCH) < S


def taps(reach):
    return [(a - 1) * PITCH * reach + (b - 1) * reach for a in range(3) for b in range(3)]


def gelu_parts(x):
    k = math.sqrt(2.0 / math.pi)
    sq = x * x
    t = jnp.tanh(k * x * (1.0 + 0.044715 * sq))
    half = 0.5 * (1.0 + t)
    slope = half + 0.5 * x * (1.0 - t * t) * (k * (1.0 + 3.0 * 0.044715 * sq))
    return x * half, slope


def gather_taps(col, wide, reach, sign, start, count):
    for n, off in enumerate(taps(reach)):
        lo = BASE + start + sign * off
        col[C * n : C * (n + 1), :] = wide[:, lo : lo + count]


def up_matrix():
    m = lax.broadcasted_iota(jnp.int32, (1, 256), 1)
    place = lax.broadcasted_iota(jnp.int32, (INNER, 256), 0)
    return jnp.where(place == 72 * (m >> 4) + 2 * (m & 15), 1.0, 0.0).astype(BF)


def load_body(codes_hbm, x_hbm, cot_hbm, edges, load, codes, x, sems):
    copies = [
        pltpu.make_async_copy(x_hbm, x, sems.at[0]),
        pltpu.make_async_copy(codes_hbm, codes, sems.at[1]),
    ]
    beside = [
        pltpu.make_async_copy(x_hbm, load.at[:, pl.ds(0, S * S)], sems.at[2]),
        pltpu.make_async_copy(cot_hbm, load.at[:, pl.ds(S * S, 256)], sems.at[3]),
    ]
    for copy in copies + beside:
        copy.start()
    lane, edge, along = lanes_of()[:3]
    y = jnp.where((edge & 1) == 0, jnp.where(edge == 0, 0, S - 1), along)
    column = jnp.where((edge & 1) == 0, along, jnp.where(edge == 1, S - 1, 0))
    hot = pick([S * y + column], 0, S * S)
    for copy in copies:
        copy.wait()
    edges[:, :SLOT] = mm(x[...], hot).astype(BF)
    row = lax.broadcasted_iota(jnp.int32, (C, SLOT), 0)
    value = jnp.where(row == 0, codes[0, 0], jnp.where(row == 1, codes[0, 1], jnp.where(row == 2, codes[0, 2], codes[0, 3])))
    edges[:, SLOT:] = value.astype(F32).astype(BF)
    for copy in beside:
        copy.wait()


def edge_row(facts, group):
    lane, _, along, part, kind, j = lanes_of()
    side, code = facts[group : group + 1, :], facts[4 + group : 5 + group, :]
    along = jnp.where((code & 1) == 1, 31 - along, along)
    place = S * ((side - code + 4) & 3) + along
    valid = lane < S
    if group >= 2:
        mine = (part >= 0) & (kind < 4) & ((kind & 1) == group - 2) & (j == 0)
        corner = jnp.where(kind >= 2, 2 * S, 0) + jnp.where(side == 1, S - 1, 0)
        place = jnp.where(mine, corner, place)
        valid = valid | mine
    return jnp.where(valid, place, -1)


def send_inputs_body(edges, facts, *slots):
    codes = edges[:16, SLOT:].astype(F32).astype(jnp.int32)
    row, column = lax.axis_index("core"), 1 - (lax.axis_index("z") & 1)
    sides = [2 - 2 * row, 2 * row, 1 + 2 * column, 3 - 2 * column]
    for g, side in enumerate(sides):
        code = jnp.where(side == 2, codes[2:3, :], codes[3:4, :])
        code = jnp.where(side == 1, codes[1:2, :], code)
        code = jnp.where(side == 0, codes[0:1, :], code)
        facts[g : g + 1, :] = jnp.full((1, SLOT), side, jnp.int32)
        facts[4 + g : 5 + g, :] = code
    hot = pick([edge_row(facts, g) for g in range(4)], 0, SLOT)
    write_slots(slots, mm(edges[:, :SLOT], hot))


def hots_body(facts, rim_one, rim_two, source_one, source_two):
    rim_one[...] = pick(rims(facts, 1), 0, FULL)
    rim_two[...] = pick(rims(facts, 2), 0, FULL)
    source_one[...] = pick(sources(facts, 1), BASE, INNER)
    source_two[...] = pick(sources(facts, 2), BASE, INNER)


def spread_body(load, one, spread, one_here):
    one_here[...] = one[...]
    spread[...] = jnp.zeros_like(spread)
    for y in range(S):
        spread[:, BASE + PITCH * y : BASE + PITCH * y + S] = load[:, S * y : S * y + S]


def transpose_taps(src, dst, count):
    for n in range(count):
        block = src[:, C * n : C * (n + 1)].astype(F32)
        dst[:, C * n : C * (n + 1)] = jnp.transpose(block).astype(BF)


def prepare_body(load, down, one, two, upstream, grad_two, one_t, two_t, wide, col, down_t):
    transpose_taps(one, one_t, 9)
    transpose_taps(two, two_t, 9)
    transpose_taps(down, down_t, 4)
    wide[...] = jnp.zeros_like(wide)
    wide[:, BASE : BASE + INNER] = nt(load[:, S * S :], up_matrix()).astype(BF)
    for n in range(4):
        lo = BASE - (n // 2) * PITCH - n % 2
        col[C * n : C * (n + 1), :] = wide[:, lo : lo + INNER]
    upstream[...] = wide[:, BASE : BASE + INNER]
    grad_two[...] = mm(down_t[...], col[...])


def first_body(rim, source, spread, r0, r1, r2, r3, w, col, hidden, slope, m3, m2, m1, m0, wide):
    halo = nt(read_slots((r0, r1, r2, r3)), rim[...]).astype(BF)
    wide[:, BASE : BASE + FULL] = spread[...] + halo
    gather_taps(col, wide, 1, 1, BASE, INNER)
    value, grad = gelu_parts(mm(w[...], col[...]))
    value = jnp.where(columns_mask(), value, 0.0).astype(BF)
    hidden[...] = value
    slope[...] = grad
    write_slots((m3, m2, m1, m0), mm(value, source[...]))


def second_body(
    rim, hidden, r0, r1, r2, r3, w, wt, grad_two,
    ext, hidden_two, delta, grad_mid, m3, m2, m1, m0, wide, col, col_full,
):
    halo = nt(read_slots((r0, r1, r2, r3)), rim[...]).astype(BF)
    wide[:, BASE : BASE + FULL] = halo
    wide[:, 2 * BASE : 2 * BASE + INNER] = halo[:, BASE : BASE + INNER] + hidden[...]
    ext[...] = wide[:, BASE : BASE + FULL]
    gather_taps(col, wide, 2, 1, BASE, INNER)
    value, grad = gelu_parts(mm(w[...], col[...]))
    hidden_two[...] = value.astype(BF)
    back = jnp.where(columns_mask(), grad * grad_two[...], 0.0).astype(BF)
    delta[...] = back
    wide[...] = jnp.zeros_like(wide)
    wide[:, 2 * BASE : 2 * BASE + INNER] = back
    gather_taps(col_full, wide, 2, -1, 0, FULL)
    pad = mm(wt[...], col_full[...])
    grad_mid[...] = pad[:, BASE : BASE + INNER]
    write_slots((m3, m2, m1, m0), mm(pad.astype(BF), rim[...]))


def second_sums_body(scale, ext, hidden_two, delta, upstream, down, encoded, grad, grad_down, wide, col):
    wide[:, BASE : BASE + FULL] = ext[...]
    gather_taps(col, wide, 2, 1, BASE, INNER)
    grad[...] = nt(delta[...], col[...]) * scale
    wide[:, 2 * BASE : 2 * BASE + INNER] = hidden_two[...]
    for n in range(4):
        lo = 2 * BASE + (n // 2) * PITCH + n % 2
        col[C * n : C * (n + 1), :] = wide[:, lo : lo + INNER]
    four = col[: 4 * C, :]
    grad_down[...] = nt(upstream[...], four) * scale
    encoded[...] = mm(mm(down[...], four).astype(BF), up_matrix()).astype(BF)


def third_body(scale, source, grad_mid, r0, r1, r2, r3, slope, col, sum_two, sum_down, delta, packed):
    back = nt(read_slots((r0, r1, r2, r3)), source[...])
    back = (grad_mid[...] + back) * slope[...]
    back = jnp.where(columns_mask(), back, 0.0).astype(BF)
    delta[...] = back
    sums = [nt(back, col[...]) * scale, sum_two[...], sum_down[...], jnp.zeros((C, SLOT), F32)]
    sums = jnp.concatenate(sums, axis=1)
    for n in range(PACKED // C):
        packed[C * n : C * (n + 1), :] = sums[:, SLOT * n : SLOT * (n + 1)].astype(BF)


def unpack_body(packed, one, two, down):
    sums = [packed[C * n : C * (n + 1), :].astype(F32) for n in range(PACKED // C - 1)]
    sums = jnp.concatenate(sums, axis=1)
    one[...] = sums[:, : 9 * C]
    two[...] = sums[:, 9 * C : 18 * C]
    down[...] = sums[:, 18 * C :]


def fourth_body(rim, delta, wt, grad, m3, m2, m1, m0, wide, col_full):
    wide[...] = jnp.zeros_like(wide)
    wide[:, 2 * BASE : 2 * BASE + INNER] = delta[...]
    gather_taps(col_full, wide, 1, -1, 0, FULL)
    pad = mm(wt[...], col_full[...])
    grad[...] = pad[:, BASE : BASE + INNER]
    write_slots((m3, m2, m1, m0), mm(pad.astype(BF), rim[...]))


def last_body(source, grad, r0, r1, r2, r3, encoded, o):
    o[:, S * S :] = encoded[...]
    back = nt(read_slots((r0, r1, r2, r3)), source[...])
    back = (grad[...] + back).astype(BF)
    for y in range(S):
        o[:, S * y : S * y + S] = back[:, PITCH * y : PITCH * y + S]


def home(t):
    row, column = t // ROW_TILES, t % ROW_TILES
    x, y = RING[row // 2]
    return ((x * 2 + y) * 8 + 7 - column) * 2 + row % 2


def move(value, pairs):
    return lax.ppermute(value, TILE, pairs)


def swap(value, step, parity):
    count = lax.axis_size(TILE)
    pairs = []
    for t in range(count):
        if (t // step) % 2 == parity:
            here, there = home(t), home((t + step) % count)
            pairs += [(here, there), (there, here)]
    return move(value, pairs)


def lane():
    return lax.broadcasted_iota(jnp.int32, (C, SLOT), 1)


def used(message):
    return jnp.where(lane() < CORNER + 16, message, 0)


def exchange(m, done=()):
    r3 = swap(used(m[3]), 1, 1)
    r2 = swap(used(m[2]), 1, 0)
    corners = jnp.where(((lane() >> 2) & 1) == 0, r2, r3)
    if done:
        corners, done = lax.optimization_barrier((corners, done))
    r1 = swap(jnp.where(lane() < CORNER, m[1], corners), ROW_TILES, 1)
    r0 = swap(jnp.where(lane() < CORNER, m[0], corners), ROW_TILES, 0)
    return (r0, r1, r2, r3), done


def north_south_back(m):
    r1 = swap(used(m[1]), ROW_TILES, 1)
    r0 = swap(used(m[0]), ROW_TILES, 0)
    return r0, r1, r0 + r1


def east_west_back(m, corners):
    r3 = swap(jnp.where(lane() < CORNER, m[3], corners), 1, 1)
    r2 = swap(jnp.where(lane() < CORNER, m[2], corners), 1, 0)
    return r2, r3


def exchange_back(m):
    r0, r1, corners = north_south_back(m)
    return (r0, r1) + east_west_back(m, corners)


def fold_body(parts, o):
    total = parts[0].astype(F32)
    for n in range(1, parts.shape[0]):
        total = total + parts[n].astype(F32)
    total = total.astype(BF)
    for n in range(o.shape[0]):
        o[n] = total


def trade(parts, axes):
    return lax.all_to_all(parts, axes, 0, 0, tiled=True)


def fold(parts):
    (spread,) = call(fold_body, [out(parts.shape, BF)], [], [parts], C * C, "fold")
    return spread


def per_device(inputs, cotangent, seam_codes, conv_one, conv_two, down_weight):
    x, cot = inputs[0, 0], cotangent[0, 0]
    assert lax.axis_size(TILE) == 128
    scale = 1.0 / math.sqrt(lax.axis_size(TILE + MEMBER) * S * S)

    slots = [out((C, SLOT), BF)] * 4
    wide, col = pltpu.VMEM((C, WIDE), BF), pltpu.VMEM((9 * C, INNER), BF)
    col_full = pltpu.VMEM((9 * C, FULL), BF)
    dense = 2 * C * 9 * C * INNER

    edges, load = call(
        load_body,
        [out((C, 2 * SLOT), BF), out((C, LOAD), BF)],
        [pltpu.SMEM((1, 4), jnp.int32), pltpu.VMEM((C, S * S), BF), pltpu.SemaphoreType.DMA((4,))],
        [seam_codes, x, cot],
        C * LOAD,
        "load",
        pltpu.HBM,
        60,
        pl.ANY,
    )
    there = [(t, home(t)) for t in range(128)]
    edges, load = move(edges, there), move(load, there)
    facts, *sent = call(
        send_inputs_body, [out((8, SLOT), jnp.int32)] + slots, [], [edges], 2 * C * SLOT * 512, "send_inputs"
    )
    hots = call(
        hots_body,
        [out((FULL, 512), BF)] * 2 + [out((INNER, 512), BF)] * 2,
        [],
        [facts],
        dense,
        "hots",
    )
    got, hots = exchange(sent[::-1], hots)
    rim_one, rim_two, source_one, source_two = hots
    spread, conv_one = call(
        spread_body, [out((C, FULL), BF), out((C, 9 * C), BF)], [], [load, conv_one], C * FULL, "spread"
    )
    upstream, grad_two, one_t, two_t = call(
        prepare_body,
        [out((C, INNER), BF), out((C, INNER), F32)] + [out((C, 9 * C), BF)] * 2,
        [wide, pltpu.VMEM((4 * C, INNER), BF), pltpu.VMEM((C, 4 * C), BF)],
        [load, down_weight, conv_one, conv_two],
        dense,
        "prepare",
    )
    taps_one, hidden, slope, *sent = call(
        first_body,
        [out((9 * C, INNER), BF), out((C, INNER), BF), out((C, INNER), F32)] + slots,
        [wide],
        [rim_one, source_two, spread, *got, conv_one],
        2 * dense,
        "first",
    )
    got, _ = exchange(sent[::-1])
    ext_two, hidden_two, delta_two, grad_mid, *sent = call(
        second_body,
        [out((C, FULL), BF), out((C, INNER), BF), out((C, INNER), BF), out((C, INNER), F32)] + slots,
        [wide, col, col_full],
        [rim_two, hidden, *got, conv_two, two_t, grad_two],
        3 * dense,
        "second",
    )
    got = exchange_back(sent[::-1])
    encoded, sum_two, sum_down = call(
        lambda *refs: second_sums_body(scale, *refs),
        [out((C, 256), BF), out((C, 9 * C), F32), out((C, 4 * C), F32)],
        [wide, col],
        [ext_two, hidden_two, delta_two, upstream, down_weight],
        2 * dense,
        "second_sums",
    )
    delta_one, packed = call(
        lambda *refs: third_body(scale, *refs),
        [out((C, INNER), BF), out((PACKED, SLOT), BF)],
        [],
        [source_two, grad_mid, *got, slope, taps_one, sum_two, sum_down],
        2 * dense,
        "third",
    )
    grad_in, *sent = call(
        fourth_body,
        [out((C, INNER), F32)] + slots,
        [wide, col_full],
        [rim_one, delta_one, one_t],
        2 * dense,
        "fourth",
    )
    assert lax.axis_size(NEAR) == lax.axis_size(FAR) == 16
    parts = trade(packed.reshape(16, PACKED // 16, SLOT), NEAR)
    sent = sent[::-1]
    r0, r1, corners = north_south_back(sent)
    parts = trade(fold(parts), FAR)
    r2, r3 = east_west_back(sent, corners)
    parts = trade(fold(parts), NEAR)
    (results,) = call(
        last_body, [out((C, LOAD), BF)], [], [source_one, grad_in, r0, r1, r2, r3, encoded], dense, "last"
    )
    results = move(results, [(home(t), t) for t in range(128)])
    sums = call(
        unpack_body,
        [out((C, 9 * C), F32), out((C, 9 * C), F32), out((C, 4 * C), F32)],
        [],
        [parts.reshape(PACKED, SLOT)],
        C * C,
        "unpack",
    )
    return (
        results[:, S * S :].reshape(1, 1, C, 256),
        results[:, : S * S].reshape(1, 1, C, S * S),
        *sums,
    )


def solution(mesh):
    axes = Mesh(mesh.devices.reshape(4, 2, 8, 2, 2), TILE + MEMBER)
    split = P(MEMBER, TILE, None, None)
    return jax.shard_map(
        per_device,
        mesh=axes,
        in_specs=(split, split, P(TILE, None), P(), P(), P()),
        out_specs=(split, split, P(), P(), P()),
        check_vma=False,
    )
```
